32 devices in a mesh: rows: 16 (over z, y, x), batch: 2 (over core).
Axes of the slice: x: 2, y: 2, z: 4, core: 2. Of those that a mesh axis runs over, the one named last changes fastest.
Arguments:
- frames: bfloat16 [4096, 1024], P('rows', 'batch'), may hold values from -40 to 40
- tap_table: int32 [63], replicated, may hold values from -128 to 127
- sketch_matrix: bfloat16 [512, 256], replicated, may hold values from -0.25 to 0.25
- decay_rates: float32 [2, 256], P('batch'), may hold values from 0.5 to 1
Outputs:
- basis: float32 [2, 4096, 256], P('batch', 'rows')
- factor: float32 [2, 256, 256], P('batch')
- coeffs: float32 [2, 256, 512], P('batch')
The draws below stay inside these ranges and needn't reach their ends.
All inputs are finite; a program needn't handle non-finite values.
Results may differ from the reference program's by a relative error of at most 0.0039.
The reference program's roundings to bfloat16 on the way count: a program that leaves them out, or rounds other values in their place, can miss the bound.
Values may be sent and summed in bfloat16 or wider, within the bound.
A program may use at most 64 MiB of HBM per device.

```python
import math
import jax
import jax.numpy as jnp
from jax import lax

FR = 512
K = 256
TAPS = 63
NBATCH = 2
NFRAMES = 1024
NPOINTS = 4096


def draw_frames(key, part):
    place = jax.lax.broadcasted_iota(jnp.float32, (NPOINTS, NFRAMES), 0) / NPOINTS
    values = jnp.clip(jax.random.normal(key, (NPOINTS, NFRAMES), jnp.float32), -4.0, 4.0)
    scale = jnp.exp(math.log(4.0) * place)
    return (values * scale).astype(jnp.bfloat16)


def place_ends(entries, key, least, high):
    shape = entries.shape
    spot = [jax.random.randint(jax.random.fold_in(key, axis), (), 0, shape[axis]) for axis in range(len(shape))]
    entries = entries.at[tuple(spot)].set(least)
    longest = shape.index(max(shape))
    spot[longest] = (spot[longest] + 1) % shape[longest]
    return entries.at[tuple(spot)].set(high)


def levels(stream_key, extent, cuts, low, top_value):
    def one(position, shards_of):
        heights = jax.random.uniform(jax.random.fold_in(jax.random.fold_in(stream_key, 6), position), (shards_of,), jnp.float32, low / len(cuts), top_value / len(cuts))
        return jnp.repeat(jnp.exp(heights), extent[position] // shards_of).reshape((-1,) + (1,) * (len(extent) - position - 1))

    gain = one(*cuts[0])
    for cut in cuts[1:]:
        gain = gain * one(*cut)
    return gain


def normal_values(rng, extent, width, most, kind=jnp.bfloat16):
    drawn = width * jax.random.normal(rng, extent, jnp.float32)
    return jnp.clip(drawn, min=-most, max=most).astype(kind)


def setup_inputs(seed: int = 0) -> dict:
    key_list = jax.random.split(jax.random.key(seed), 5)
    frames = draw_frames(jax.random.fold_in(key_list[4], 71), 0)
    tap_table = place_ends(jax.random.randint(key_list[1], (TAPS,), -128, 128), jax.random.fold_in(key_list[1], 1), -128, 127).astype(jnp.int32)
    sketch_matrix = normal_values(key_list[2], (FR, K), FR ** -0.5, 0.25)
    decay_rates = jnp.clip(0.5 + 0.5 * jax.random.uniform(key_list[3], (NBATCH, K), jnp.float32) ** levels(key_list[3], (NBATCH, K), ((0, 2),), -0.2, 0.2), 0.5, 1.0)
    return dict(frames=frames, tap_table=tap_table, sketch_matrix=sketch_matrix, decay_rates=decay_rates)


HIGH = lax.Precision.HIGHEST

def band_matrix(coefs, rows_count, cols_count, offset):
    row_ids = lax.broadcasted_iota(jnp.int32, (rows_count, cols_count), 0)
    col_ids = lax.broadcasted_iota(jnp.int32, (rows_count, cols_count), 1)
    lag_ids = col_ids - row_ids + offset
    valid = (lag_ids >= 0) & (lag_ids < coefs.shape[0])
    values = jnp.take(coefs, jnp.clip(lag_ids, 0, coefs.shape[0] - 1))
    return jnp.where(valid, values, jnp.zeros_like(values))

def gram_of(block):
    return lax.dot_general(block.astype(jnp.float32), block.astype(jnp.float32), (((0,), (0,)), ((), ())), precision=HIGH, preferred_element_type=jnp.float32)

def reference(frames, tap_table, sketch_matrix, decay_rates):
    npoints = frames.shape[0]
    nbatch = decay_rates.shape[0]
    coefs = (tap_table.astype(jnp.float32) / 1024.0).astype(jnp.bfloat16).astype(jnp.float32)
    main_band = band_matrix(coefs, FR, FR, 0)
    hist_band = band_matrix(coefs, TAPS - 1, FR, TAPS - 1)
    blocks = jnp.transpose(frames.reshape(npoints, nbatch, FR), (1, 0, 2))
    histories = jnp.concatenate([jnp.zeros((1, npoints, TAPS - 1), frames.dtype), blocks[:-1, :, FR - (TAPS - 1):]], axis=0)
    sketch_wide = sketch_matrix.astype(jnp.float32)
    root_points = math.sqrt(npoints)

    def section(carried, inputs):
        block, history, rates = inputs
        filtered = (jnp.dot(block.astype(jnp.float32), main_band, precision=HIGH) + jnp.dot(history.astype(jnp.float32), hist_band, precision=HIGH)).astype(jnp.bfloat16)
        sketched = jnp.dot(filtered.astype(jnp.float32), sketch_wide, precision=HIGH)
        weighted = rates[None, :] * carried + sketched
        lower_one = jnp.linalg.cholesky(gram_of(weighted))
        final_q = lax.linalg.triangular_solve(lower_one, weighted, left_side=False, lower=True, transpose_a=True)
        scaled = final_q * root_points
        projected = lax.dot_general(scaled.astype(jnp.float32), filtered.astype(jnp.float32), (((0,), (0,)), ((), ())), precision=HIGH, preferred_element_type=jnp.float32)
        projected = projected * (math.sqrt(K) / npoints)
        return (weighted, (scaled, lower_one.T / root_points, projected))
    start = jnp.zeros((npoints, K), jnp.float32)
    last, outputs = lax.scan(section, start, (blocks, histories, decay_rates))
    return (outputs[0], outputs[1], outputs[2])
```

```python
import functools
import math

import jax
import jax.numpy as jnp
from jax import lax
from jax.experimental import pallas as pl
from jax.experimental.pallas import tpu as pltpu
from jax.sharding import PartitionSpec as P

MESH = pl.DeviceIdType.MESH
HIGHEST = lax.Precision.HIGHEST
F32 = jnp.float32
BF16 = jnp.bfloat16
LANES = 128
PANEL = 8
VMEM_SPEC = pl.BlockSpec(memory_space=pltpu.VMEM)


def greet(count, batches, with_batch):
    row, turn = lax.axis_index("rows"), lax.axis_index("batch")
    barrier = pltpu.get_barrier_semaphore()
    for step in range(1, count):
        pl.semaphore_signal(
            barrier, inc=1, device_id=(lax.rem(row + step, count), turn), device_id_type=MESH
        )
    waits = count - 1
    if with_batch and batches > 1:

        @pl.when(turn > 0)
        def _():
            pl.semaphore_signal(barrier, inc=1, device_id=(row, turn - 1), device_id_type=MESH)

        @pl.when(turn < batches - 1)
        def _():
            pl.semaphore_signal(barrier, inc=1, device_id=(row, turn + 1), device_id_type=MESH)

        waits = waits + jnp.where(turn > 0, 1, 0) + jnp.where(turn < batches - 1, 1, 0)
    pl.semaphore_wait(barrier, waits)


def exchange(count, source_of, target_of, send_sems, recv_sems):
    row, turn = lax.axis_index("rows"), lax.axis_index("batch")
    copies = []
    for step in range(1, count):
        peer = lax.rem(row + step, count)
        copy = pltpu.make_async_remote_copy(
            src_ref=source_of(peer),
            dst_ref=target_of(row),
            send_sem=send_sems.at[step],
            recv_sem=recv_sems.at[step],
            device_id=(peer, turn),
            device_id_type=MESH,
        )
        copy.start()
        copies.append(copy)
    return copies


def sum_over_rows(count, parts, landed, total, send_a, recv_a, send_b, recv_b):
    row = lax.axis_index("rows")
    first = exchange(
        count, lambda peer: parts.at[peer], lambda mine: landed.at[mine], send_a, recv_a
    )
    landed[row] = parts[row]
    for copy in first:
        copy.wait_recv()
    summed = landed[0].astype(F32)
    for sender in range(1, count):
        summed = summed + landed[sender].astype(F32)
    total[row] = summed.astype(total.dtype)
    second = exchange(
        count, lambda peer: total.at[row], lambda mine: total.at[mine], send_b, recv_b
    )
    for copy in second:
        copy.wait_recv()
    for copy in first + second:
        copy.wait_send()


def sketch_kernel(
    count, batches, shard,
    frames, taps, sketch, rates, gram_out, weighted, filtered,
    tap_row, history, before, parts, landed, total, hist_sems, prev_sems, send_a, recv_a, send_b, recv_b,
):
    row, turn = lax.axis_index("rows"), lax.axis_index("batch")
    frame_count = frames.shape[1]
    rank = sketch.shape[1]
    greet(count, batches, True)

    def hist_copy():
        return pltpu.make_async_remote_copy(
            src_ref=frames.at[:, pl.ds(frame_count - LANES, LANES)],
            dst_ref=history,
            send_sem=hist_sems.at[0],
            recv_sem=hist_sems.at[1],
            device_id=(row, turn + 1),
            device_id_type=MESH,
        )

    def prev_copy():
        return pltpu.make_async_remote_copy(
            src_ref=weighted,
            dst_ref=before,
            send_sem=prev_sems.at[0],
            recv_sem=prev_sems.at[1],
            device_id=(row, turn + 1),
            device_id_type=MESH,
        )

    @pl.when(turn < batches - 1)
    def _():
        hist_copy().start()

    tap_row[...] = jnp.zeros_like(tap_row)
    tap_row[:, : taps.shape[1]] = taps[...].astype(F32) / 1024.0
    spread = jnp.broadcast_to(tap_row[...], (LANES, tap_row.shape[1]))
    rolled = pltpu.roll(spread, 0, 1, stride=1, stride_axis=0)
    wide = tap_row.shape[1]
    after = jnp.concatenate([rolled[:, wide - LANES :], rolled[:, :LANES]], axis=1)
    band = jnp.concatenate([rolled[:, LANES : 3 * LANES], rolled[:, : 2 * LANES], after], axis=0).astype(BF16)

    step = 2 * LANES
    for start in range(step, frame_count, step):
        filtered[:, start : start + step] = jnp.dot(
            frames[:, start - LANES : start + step], band, preferred_element_type=F32
        ).astype(BF16)
    here = jnp.dot(frames[:, :step], band[LANES:], preferred_element_type=F32)

    @pl.when(turn == 0)
    def _():
        history[...] = jnp.zeros_like(history)

    @pl.when(turn > 0)
    def _():
        hist_copy().wait_recv()

    filtered[:, :step] = (
        here + jnp.dot(history[...], band[:LANES], preferred_element_type=F32)
    ).astype(BF16)
    sketched = jnp.dot(filtered[...], sketch[...], preferred_element_type=F32)
    weighted[...] = sketched

    @pl.when(turn > 0)
    def _():
        prev_copy().wait_recv()
        weighted[...] = rates[...] * before[...] + weighted[...]

    @pl.when(turn < batches - 1)
    def _():
        prev_copy().start()

    value = weighted[...]
    gram = jnp.dot(value.T, value, precision=HIGHEST, preferred_element_type=F32)
    half = rank // 2
    blocks = [gram[:half, :half], gram[:half, half:], gram[half:, half:]]
    packed = jnp.concatenate(blocks, axis=0)
    for index in range(count):
        low = index * shard
        if low < packed.shape[0]:
            parts[index] = packed[low : low + shard]
        else:
            parts[index] = jnp.zeros((shard, half), F32)
    sum_over_rows(count, parts, landed, total, send_a, recv_a, send_b, recv_b)
    for index in range(count):
        low = index * shard
        if low < packed.shape[0]:
            gram_out[low : low + shard] = total[index]

    @pl.when(turn < batches - 1)
    def _():
        hist_copy().wait_send()
        prev_copy().wait_send()


def pieces(x):
    high = x.astype(BF16).astype(F32)
    rest = x - high
    mid = rest.astype(BF16).astype(F32)
    return high, mid, rest - mid


def eliminate(work, upper, inverse, begin, wide):
    rank = work.shape[0]
    first = begin
    last = rank + begin + LANES

    def panel(index, _):
        offset = pl.multiple_of(index * PANEL, PANEL)
        rows = pl.ds(pl.multiple_of(begin + offset, PANEL), PANEL)
        block = work[rows, first:last]
        corner = pltpu.roll(block[:, :LANES], lax.rem(LANES - offset, LANES), 1)
        full = (PANEL, LANES)
        columns = [jnp.broadcast_to(corner[:, j : j + 1], full) for j in range(PANEL)]
        held = {
            (i, j): jnp.broadcast_to(columns[j][i : i + 1], full)
            for j in range(PANEL)
            for i in range(j, PANEL)
        }
        lines = [jnp.broadcast_to(block[i : i + 1], block.shape) for i in range(PANEL)]
        copies = block.shape[1] // LANES
        place = lax.broadcasted_iota(jnp.int32, block.shape, 0)
        result = jnp.zeros_like(block)
        for j in range(PANEL):
            scale = lax.rsqrt(held[j, j])
            factors = {i: held[i, j] * scale for i in range(j + 1, PANEL)}
            for i in range(j + 1, PANEL):
                for k in range(j + 1, i + 1):
                    held[i, k] = held[i, k] - factors[i] * factors[k]
            done = lines[j] * jnp.concatenate([scale] * copies, axis=1)
            for i in range(j + 1, PANEL):
                lines[i] = lines[i] - jnp.concatenate([factors[i]] * copies, axis=1) * done
            result = jnp.where(place == j, done, result)
        upper[rows, first:rank] = result[:, : rank - first]
        inverse[rows, : begin + LANES] = result[:, rank - first :]
        high, mid, low = pieces(result)
        width = rank - first
        left = jnp.concatenate([high, high, mid, high, mid, low], axis=0)[:, :width].astype(BF16)
        right = jnp.concatenate([high, mid, high, low, mid, high], axis=0).astype(BF16)
        work[first:, first:last] = work[first:, first:last] - lax.dot_general(
            left, right, (((0,), (0,)), ((), ())), preferred_element_type=F32
        )
        return 0

    lax.fori_loop(0, LANES // PANEL, panel, 0)


def factor_kernel(npoints, gram, weighted, filtered, basis, factor, partial, work, upper, inverse):
    rank = weighted.shape[1]
    half = rank // 2
    across = gram[half:rank, :]
    work[:half, :half] = gram[:half, :]
    work[:half, half:rank] = across
    work[half:, :half] = across.T
    work[half:, half:rank] = gram[rank:, :]
    ids = lax.broadcasted_iota(jnp.int32, (rank, rank), 0)
    cols = lax.broadcasted_iota(jnp.int32, (rank, rank), 1)
    work[:, rank:] = jnp.where(ids == cols, 1.0, 0.0).astype(F32)
    upper[...] = jnp.zeros_like(upper)
    inverse[...] = jnp.zeros_like(inverse)
    for begin in range(0, rank, LANES):
        eliminate(work, upper, inverse, begin, LANES)
    root = math.sqrt(npoints)
    factor[0] = jnp.where(cols >= ids, upper[...], 0.0) * (1.0 / root)
    scaled = lax.dot_general(
        weighted[...], inverse[...], (((1,), (1,)), ((), ())), precision=HIGHEST, preferred_element_type=F32
    ) * root
    basis[0] = scaled
    high = scaled.astype(BF16)
    low = (scaled - high.astype(F32)).astype(BF16)
    turned = filtered[...].T
    cross = jnp.dot(turned, high, preferred_element_type=F32) + jnp.dot(turned, low, preferred_element_type=F32)
    partial[...] = (cross * (math.sqrt(rank) / npoints)).astype(partial.dtype)


def coeffs_kernel(count, batches, shard, partial, out, parts, landed, total, send_a, recv_a, send_b, recv_b):
    greet(count, batches, False)
    for index in range(count):
        low = index * shard
        if low < partial.shape[0]:
            parts[index] = partial[low : low + shard]
        else:
            parts[index] = jnp.zeros((shard, partial.shape[1]), partial.dtype)
    sum_over_rows(count, parts, landed, total, send_a, recv_a, send_b, recv_b)
    for index in range(count):
        low = index * shard
        if low < partial.shape[0]:
            out[low : low + shard] = total[index]


def shard_rows(length, count, tile):
    return tile * -(-length // (tile * count))


def sems(count):
    return [pltpu.SemaphoreType.DMA((count,)) for _ in range(4)]


def shards(frames, tap_table, sketch_matrix, decay_rates):
    count, batches = lax.axis_size("rows"), lax.axis_size("batch")
    rows_here, frame_count = frames.shape
    rank = sketch_matrix.shape[1]
    half = rank // 2
    npoints = rows_here * count
    shard = shard_rows(3 * half, count, 8)
    slots = (count, shard, half)
    limit = 48 * 1024 * 1024
    gram, weighted, filtered = pl.pallas_call(
        functools.partial(sketch_kernel, count, batches, shard),
        out_shape=(
            jax.ShapeDtypeStruct((3 * half, half), F32),
            jax.ShapeDtypeStruct((rows_here, rank), F32),
            jax.ShapeDtypeStruct((rows_here, frame_count), BF16),
        ),
        in_specs=[VMEM_SPEC] * 4,
        out_specs=(VMEM_SPEC,) * 3,
        scratch_shapes=[
            pltpu.VMEM((1, 4 * LANES), F32),
            pltpu.VMEM((rows_here, LANES), BF16),
            pltpu.VMEM((rows_here, rank), F32),
            pltpu.VMEM(slots, F32),
            pltpu.VMEM(slots, F32),
            pltpu.VMEM(slots, F32),
            pltpu.SemaphoreType.DMA((2,)),
            pltpu.SemaphoreType.DMA((2,)),
        ] + sems(count),
        compiler_params=pltpu.CompilerParams(
            collective_id=0, has_side_effects=True, vmem_limit_bytes=limit
        ),
        name="sketch",
    )(frames, tap_table.reshape(1, -1), sketch_matrix, decay_rates)
    basis, factor, partial = pl.pallas_call(
        functools.partial(factor_kernel, npoints),
        out_shape=(
            jax.ShapeDtypeStruct((1, rows_here, rank), F32),
            jax.ShapeDtypeStruct((1, rank, rank), F32),
            jax.ShapeDtypeStruct((frame_count, rank), BF16),
        ),
        in_specs=[VMEM_SPEC] * 3,
        out_specs=(VMEM_SPEC,) * 3,
        scratch_shapes=[
            pltpu.VMEM((rank, 2 * rank), F32),
            pltpu.VMEM((rank, rank), F32),
            pltpu.VMEM((rank, rank), F32),
        ],
        compiler_params=pltpu.CompilerParams(vmem_limit_bytes=limit),
        name="factor",
    )(gram, weighted, filtered)
    shard = shard_rows(frame_count, count, 16)
    slots = (count, shard, rank)
    turned = pl.pallas_call(
        functools.partial(coeffs_kernel, count, batches, shard),
        out_shape=jax.ShapeDtypeStruct((frame_count, rank), BF16),
        in_specs=[VMEM_SPEC],
        out_specs=VMEM_SPEC,
        scratch_shapes=[pltpu.VMEM(slots, BF16)] * 3 + sems(count),
        compiler_params=pltpu.CompilerParams(
            collective_id=1, has_side_effects=True, vmem_limit_bytes=limit
        ),
        name="coeffs",
    )(partial)
    return (basis, factor, turned.T.astype(F32)[None])


def solution(mesh):
    placed = (P("rows", "batch"), P(), P(), P("batch", None))
    return jax.shard_map(
        shards,
        mesh=mesh,
        in_specs=placed,
        out_specs=(P("batch", "rows", None), P("batch", None, None), P("batch", None, None)),
        check_vma=False,
    )
```

```python
import functools
import math

import jax
import jax.numpy as jnp
from jax import lax
from jax.experimental import pallas as pl
from jax.experimental.pallas import tpu as pltpu
from jax.sharding import PartitionSpec as P

MESH = pl.DeviceIdType.MESH
HIGHEST = lax.Precision.HIGHEST
F32 = jnp.float32
BF16 = jnp.bfloat16
LANES = 128
PANEL = 32
TILE = 8
VMEM_SPEC = pl.BlockSpec(memory_space=pltpu.VMEM)


def greet(count, batches, with_batch):
    row, turn = lax.axis_index("rows"), lax.axis_index("batch")
    barrier = pltpu.get_barrier_semaphore()
    for step in range(1, count):
        pl.semaphore_signal(
            barrier, inc=1, device_id=(lax.rem(row + step, count), turn), device_id_type=MESH
        )
    waits = count - 1
    if with_batch and batches > 1:

        @pl.when(turn > 0)
        def _():
            pl.semaphore_signal(barrier, inc=1, device_id=(row, turn - 1), device_id_type=MESH)

        @pl.when(turn < batches - 1)
        def _():
            pl.semaphore_signal(barrier, inc=1, device_id=(row, turn + 1), device_id_type=MESH)

        waits = waits + jnp.where(turn > 0, 1, 0) + jnp.where(turn < batches - 1, 1, 0)
    pl.semaphore_wait(barrier, waits)


def exchange(count, source_of, target_of, send_sems, recv_sems):
    row, turn = lax.axis_index("rows"), lax.axis_index("batch")
    copies = []
    for step in range(1, count):
        peer = lax.rem(row + step, count)
        copy = pltpu.make_async_remote_copy(
            src_ref=source_of(peer),
            dst_ref=target_of(row),
            send_sem=send_sems.at[step],
            recv_sem=recv_sems.at[step],
            device_id=(peer, turn),
            device_id_type=MESH,
        )
        copy.start()
        copies.append(copy)
    return copies


def fill(parts, value):
    count, shard = parts.shape[0], parts.shape[1]
    for index in range(count):
        low = index * shard
        if low < value.shape[0]:
            parts[index] = value[low : low + shard]
        else:
            parts[index] = jnp.zeros((shard, value.shape[1]), parts.dtype)


def sum_landed(parts, landed, copies):
    row = lax.axis_index("rows")
    landed[row] = parts[row]
    for copy in copies:
        copy.wait_recv()
    summed = landed[0]
    for sender in range(1, parts.shape[0]):
        summed = summed + landed[sender]
    return summed


def whole_kernel(
    count, batches, npoints,
    frames_hbm, taps_hbm, sketch_hbm, rates_hbm, basis, factor, coeffs,
    frames, taps, sketch, rates, tap_row, history, before, weighted, filtered,
    parts, landed, total, cross_parts, cross_landed, cross_total, work, upper, inverse,
    load_sems, hist_sems, prev_sems, gram_a, gram_b, gram_c, gram_d, cross_a, cross_b, cross_c, cross_d,
):
    row, turn = lax.axis_index("rows"), lax.axis_index("batch")
    frame_count = frames.shape[1]
    rank = sketch.shape[1]
    loads = [
        pltpu.make_async_copy(source, target, load_sems.at[index])
        for index, (source, target) in enumerate(
            ((taps_hbm, taps), (frames_hbm, frames), (sketch_hbm, sketch), (rates_hbm, rates))
        )
    ]
    for load in loads:
        load.start()
    greet(count, batches, True)

    def hist_copy():
        return pltpu.make_async_remote_copy(
            src_ref=frames_hbm.at[:, pl.ds(frame_count - LANES, LANES)],
            dst_ref=history,
            send_sem=hist_sems.at[0],
            recv_sem=hist_sems.at[1],
            device_id=(row, turn + 1),
            device_id_type=MESH,
        )

    def prev_copy():
        return pltpu.make_async_remote_copy(
            src_ref=weighted,
            dst_ref=before,
            send_sem=prev_sems.at[0],
            recv_sem=prev_sems.at[1],
            device_id=(row, turn + 1),
            device_id_type=MESH,
        )

    @pl.when(turn < batches - 1)
    def _():
        hist_copy().start()

    loads[0].wait()
    tap_row[...] = jnp.zeros_like(tap_row)
    tap_row[:, : taps.shape[1]] = taps[...].astype(F32) / 1024.0
    spread = jnp.broadcast_to(tap_row[...], (LANES, tap_row.shape[1]))
    rolled = pltpu.roll(spread, 0, 1, stride=1, stride_axis=0)
    wide = tap_row.shape[1]
    after = jnp.concatenate([rolled[:, wide - LANES :], rolled[:, :LANES]], axis=1)
    band = jnp.concatenate([rolled[:, LANES : 3 * LANES], rolled[:, : 2 * LANES], after], axis=0).astype(BF16)

    step = 2 * LANES
    loads[1].wait()
    for start in range(step, frame_count, step):
        filtered[:, start : start + step] = jnp.dot(
            frames[:, start - LANES : start + step], band, preferred_element_type=F32
        ).astype(BF16)
    here = jnp.dot(frames[:, :step], band[LANES:], preferred_element_type=F32)
    loads[2].wait()
    loads[3].wait()

    @pl.when(turn == 0)
    def _():
        history[...] = jnp.zeros_like(history)

    @pl.when(turn > 0)
    def _():
        hist_copy().wait_recv()

    filtered[:, :step] = (
        here + jnp.dot(history[...], band[:LANES], preferred_element_type=F32)
    ).astype(BF16)
    weighted[...] = jnp.dot(filtered[...], sketch[...], preferred_element_type=F32)

    @pl.when(turn > 0)
    def _():
        prev_copy().wait_recv()
        weighted[...] = rates[...] * before[...] + weighted[...]

    @pl.when(turn < batches - 1)
    def _():
        prev_copy().start()

    value = weighted[...]
    gram = jnp.dot(value.T, value, precision=HIGHEST, preferred_element_type=F32)
    half = rank // 2
    fill(parts, jnp.concatenate([gram[:half, :half], gram[:half, half:], gram[half:, half:]], axis=0))
    gram_first = exchange(count, lambda peer: parts.at[peer], lambda mine: landed.at[mine], gram_a, gram_b)

    turned = filtered[...].T
    cross = jnp.zeros((frame_count, rank), F32)
    for piece in reversed(pieces(value)):
        cross = cross + jnp.dot(turned, piece.astype(BF16), preferred_element_type=F32)
    fill(cross_parts, cross)

    total[row] = sum_landed(parts, landed, gram_first)
    gram_second = exchange(count, lambda peer: total.at[row], lambda mine: total.at[mine], gram_c, gram_d)
    cross_first = exchange(
        count, lambda peer: cross_parts.at[peer], lambda mine: cross_landed.at[mine], cross_a, cross_b
    )
    ids = lax.broadcasted_iota(jnp.int32, (rank, rank), 0)
    cols = lax.broadcasted_iota(jnp.int32, (rank, rank), 1)
    work[:, rank:] = jnp.where(ids == cols, 1.0, 0.0).astype(F32)
    upper[...] = jnp.zeros_like(upper)
    inverse[...] = jnp.zeros_like(inverse)
    for copy in gram_second:
        copy.wait_recv()
    packed = jnp.concatenate([total[index] for index in range(count)], axis=0)
    across = packed[half:rank]
    work[:half, :half] = packed[:half]
    work[:half, half:rank] = across
    work[half:, :half] = across.T
    work[half:, half:rank] = packed[rank : rank + half]
    for begin in range(0, rank, LANES):
        eliminate(work, upper, inverse, begin)

    root = math.sqrt(npoints)
    against = (((1,), (1,)), ((), ()))
    mine = sum_landed(cross_parts, cross_landed, cross_first) * (math.sqrt(rank) / root)
    cross_total[row] = lax.dot_general(
        mine, inverse[...], against, precision=HIGHEST, preferred_element_type=F32
    ).astype(BF16)
    cross_second = exchange(
        count, lambda peer: cross_total.at[row], lambda mine: cross_total.at[mine], cross_c, cross_d
    )
    factor[0] = jnp.where(cols >= ids, upper[...], 0.0) * (1.0 / root)
    basis[0] = lax.dot_general(
        weighted[...], inverse[...], against, precision=HIGHEST, preferred_element_type=F32
    ) * root
    for copy in cross_second:
        copy.wait_recv()
    shard = cross_total.shape[1]
    for index in range(count):
        low = index * shard
        if low < frame_count:
            coeffs[low : low + shard] = cross_total[index]

    for copy in gram_first + gram_second + cross_first + cross_second:
        copy.wait_send()

    @pl.when(turn < batches - 1)
    def _():
        hist_copy().wait_send()
        prev_copy().wait_send()


def pieces(x):
    high = x.astype(BF16).astype(F32)
    rest = x - high
    mid = rest.astype(BF16).astype(F32)
    return high, mid, rest - mid


def eliminate(work, upper, inverse, begin):
    rank = work.shape[0]
    first = begin
    last = rank + begin + LANES
    width = rank - first
    tiles = PANEL // TILE
    full = (TILE, LANES)

    def wide(x, copies):
        return jnp.concatenate([x] * copies, axis=1)

    def panel(index, _):
        offset = pl.multiple_of(index * PANEL, PANEL)
        rows = pl.ds(pl.multiple_of(begin + offset, PANEL), PANEL)
        block = work[rows, first:last]
        corner = pltpu.roll(block[:, :LANES], lax.rem(LANES - offset, LANES), 1)
        block = jnp.concatenate([block, corner], axis=1)
        copies = block.shape[1] // LANES
        body = [block[b * TILE : (b + 1) * TILE] for b in range(tiles)]
        place = lax.broadcasted_iota(jnp.int32, body[0].shape, 0)
        for c in range(tiles):
            columns = [
                [
                    jnp.broadcast_to(body[b][:, at : at + 1], full)
                    for at in range(last - first + c * TILE, last - first + (c + 1) * TILE)
                ]
                for b in range(c, tiles)
            ]
            held = {
                (i, j): jnp.broadcast_to(columns[0][j][i : i + 1], full)
                for j in range(TILE)
                for i in range(j, TILE)
            }
            lines = [jnp.broadcast_to(body[c][i : i + 1], body[c].shape) for i in range(TILE)]
            result = jnp.zeros_like(body[c])
            for j in range(TILE):
                scale = lax.rsqrt(held[j, j])
                factors = {i: held[i, j] * scale for i in range(j + 1, TILE)}
                for i in range(j + 1, TILE):
                    for k in range(j + 1, i + 1):
                        held[i, k] = held[i, k] - factors[i] * factors[k]
                done = lines[j] * wide(scale, copies)
                for i in range(j + 1, TILE):
                    lines[i] = lines[i] - wide(factors[i], copies) * done
                for b in range(c + 1, tiles):
                    down = columns[b - c][j] * scale
                    for k in range(j + 1, TILE):
                        columns[b - c][k] = columns[b - c][k] - down * factors[k]
                    body[b] = body[b] - wide(down, copies) * done
                result = jnp.where(place == j, done, result)
            body[c] = result
        solved = jnp.concatenate(body, axis=0)[:, : last - first]
        upper[rows, first:rank] = solved[:, :width]
        inverse[rows, : begin + LANES] = solved[:, width:]
        high, mid, low = pieces(solved)
        left = jnp.concatenate([high, high, mid, high, mid, low], axis=0)[:, :width].astype(BF16)
        right = jnp.concatenate([high, mid, high, low, mid, high], axis=0).astype(BF16)
        work[first:, first:last] = work[first:, first:last] - lax.dot_general(
            left, right, (((0,), (0,)), ((), ())), preferred_element_type=F32
        )
        return 0

    lax.fori_loop(0, LANES // PANEL, panel, 0)


def shard_rows(length, count, tile):
    return tile * -(-length // (tile * count))


def shards(frames, tap_table, sketch_matrix, decay_rates):
    count, batches = lax.axis_size("rows"), lax.axis_size("batch")
    rows_here, frame_count = frames.shape
    rank = sketch_matrix.shape[1]
    half = rank // 2
    taps = tap_table.reshape(1, -1)
    gram_slots = pltpu.VMEM((count, shard_rows(3 * half, count, 8), half), F32)
    cross_shard = (count, shard_rows(frame_count, count, 16), rank)
    basis, factor, coeffs = pl.pallas_call(
        functools.partial(whole_kernel, count, batches, rows_here * count),
        out_shape=(
            jax.ShapeDtypeStruct((1, rows_here, rank), F32),
            jax.ShapeDtypeStruct((1, rank, rank), F32),
            jax.ShapeDtypeStruct((frame_count, rank), BF16),
        ),
        in_specs=[pl.BlockSpec(memory_space=pltpu.HBM)] * 4,
        out_specs=(VMEM_SPEC,) * 3,
        scratch_shapes=[
            pltpu.VMEM(frames.shape, BF16),
            pltpu.VMEM(taps.shape, jnp.int32),
            pltpu.VMEM(sketch_matrix.shape, BF16),
            pltpu.VMEM(decay_rates.shape, F32),
            pltpu.VMEM((1, 4 * LANES), F32),
            pltpu.VMEM((rows_here, LANES), BF16),
            pltpu.VMEM((rows_here, rank), F32),
            pltpu.VMEM((rows_here, rank), F32),
            pltpu.VMEM((rows_here, frame_count), BF16),
            gram_slots,
            gram_slots,
            gram_slots,
            pltpu.VMEM(cross_shard, F32),
            pltpu.VMEM(cross_shard, F32),
            pltpu.VMEM(cross_shard, BF16),
            pltpu.VMEM((rank, 2 * rank), F32),
            pltpu.VMEM((rank, rank), F32),
            pltpu.VMEM((rank, rank), F32),
            pltpu.SemaphoreType.DMA((4,)),
            pltpu.SemaphoreType.DMA((2,)),
            pltpu.SemaphoreType.DMA((2,)),
        ] + [pltpu.SemaphoreType.DMA((count,)) for _ in range(8)],
        compiler_params=pltpu.CompilerParams(
            collective_id=0, has_side_effects=True, vmem_limit_bytes=48 * 1024 * 1024
        ),
        name="whole",
    )(frames, taps, sketch_matrix, decay_rates)
    return (basis, factor, coeffs.T.astype(F32)[None])


def solution(mesh):
    placed = (P("rows", "batch"), P(), P(), P("batch", None))
    return jax.shard_map(
        shards,
        mesh=mesh,
        in_specs=placed,
        out_specs=(P("batch", "rows", None), P("batch", None, None), P("batch", None, None)),
        check_vma=False,
    )
```

```python
import functools
import math

import jax
import jax.numpy as jnp
from jax import lax
from jax.experimental import pallas as pl
from jax.experimental.pallas import tpu as pltpu
from jax.sharding import PartitionSpec as P

MESH = pl.DeviceIdType.MESH
HIGHEST = lax.Precision.HIGHEST
F32 = jnp.float32
BF16 = jnp.bfloat16
LANES = 128
PANEL = 32
TILE = 8
GRANT = 63 * 1024 * 1024
HBM_SPEC = pl.BlockSpec(memory_space=pltpu.HBM)
VMEM_SPEC = pl.BlockSpec(memory_space=pltpu.VMEM)


def greet(count, batches, with_batch):
    row, turn = lax.axis_index("rows"), lax.axis_index("batch")
    barrier = pltpu.get_barrier_semaphore()
    for step in range(1, count):
        pl.semaphore_signal(
            barrier, inc=1, device_id=(lax.rem(row + step, count), turn), device_id_type=MESH
        )
    waits = count - 1
    if with_batch and batches > 1:

        @pl.when(turn > 0)
        def _():
            pl.semaphore_signal(barrier, inc=1, device_id=(row, turn - 1), device_id_type=MESH)

        @pl.when(turn < batches - 1)
        def _():
            pl.semaphore_signal(barrier, inc=1, device_id=(row, turn + 1), device_id_type=MESH)

        waits = waits + jnp.where(turn > 0, 1, 0) + jnp.where(turn < batches - 1, 1, 0)
    pl.semaphore_wait(barrier, waits)


def exchange(count, source_of, target_of, send_sems, recv_sems):
    row, turn = lax.axis_index("rows"), lax.axis_index("batch")
    copies = []
    for step in range(1, count):
        peer = lax.rem(row + step, count)
        copy = pltpu.make_async_remote_copy(
            src_ref=source_of(peer),
            dst_ref=target_of(row),
            send_sem=send_sems.at[step],
            recv_sem=recv_sems.at[step],
            device_id=(peer, turn),
            device_id_type=MESH,
        )
        copy.start()
        copies.append(copy)
    return copies


def groups(count):
    inner = 4 if count % 4 == 0 else 1
    return count // inner, inner


def send(source, target, send_sems, recv_sems, index, peer):
    copy = pltpu.make_async_remote_copy(
        src_ref=source,
        dst_ref=target,
        send_sem=send_sems.at[index],
        recv_sem=recv_sems.at[index],
        device_id=(peer, lax.axis_index("batch")),
        device_id_type=MESH,
    )
    copy.start()
    return copy


def place_of(count):
    inner = groups(count)[1]
    row = lax.axis_index("rows")
    return lax.div(row, inner), lax.rem(row, inner)


def gather(count, total, send_sems, recv_sems):
    outer, inner = groups(count)
    plane, spot = place_of(count)
    row = lax.axis_index("rows")
    across, within = [], []
    for o in range(1, outer):
        peer = lax.rem(plane + o, outer) * inner + spot
        across.append(send(total.at[row], total.at[row], send_sems, recv_sems, o * inner, peer))
    for o in range(outer):
        if o > 0:
            across[o - 1].wait_recv()
        owner = lax.rem(plane - o + outer, outer) * inner + spot
        for i in range(1, inner):
            peer = plane * inner + lax.rem(spot + i, inner)
            within.append(send(total.at[owner], total.at[owner], send_sems, recv_sems, o * inner + i, peer))
    return across, within


def cut(value, index, shard, dtype):
    low = index * shard
    if low < value.shape[0]:
        return value[low : low + shard]
    return jnp.zeros((shard, value.shape[1]), dtype)


def sum_slots(landed, copies):
    for copy in copies:
        copy.wait_recv()
    summed = landed[0]
    for sender in range(1, landed.shape[0]):
        summed = summed + landed[sender]
    return summed


def whole_kernel(
    count, batches, npoints,
    frames_hbm, taps_hbm, sketch_hbm, rates_hbm, basis_hbm, factor_hbm, coeffs,
    frames, taps, sketch, rates, tap_row, history, before, weighted, filtered,
    parts, landed, total, cross_parts, cross_landed, cross_mid, cross_last, cross_total, work, upper, inverse, basis, factor,
    load_sems, store_sems, hist_sems, prev_sems, gram_a, gram_b, gram_c, gram_d, cross_a, cross_b, cross_c, cross_d, cross_e, cross_f,
):
    row, turn = lax.axis_index("rows"), lax.axis_index("batch")
    frame_count = frames.shape[1]
    rank = sketch.shape[1]
    loads = [
        pltpu.make_async_copy(source, target, load_sems.at[index])
        for index, (source, target) in enumerate(
            ((taps_hbm, taps), (frames_hbm, frames), (sketch_hbm, sketch), (rates_hbm, rates))
        )
    ]
    for load in loads:
        load.start()
    greet(count, batches, True)

    def hist_copy():
        return pltpu.make_async_remote_copy(
            src_ref=frames_hbm.at[:, pl.ds(frame_count - LANES, LANES)],
            dst_ref=history,
            send_sem=hist_sems.at[0],
            recv_sem=hist_sems.at[1],
            device_id=(row, turn + 1),
            device_id_type=MESH,
        )

    def prev_copy():
        return pltpu.make_async_remote_copy(
            src_ref=weighted,
            dst_ref=before,
            send_sem=prev_sems.at[0],
            recv_sem=prev_sems.at[1],
            device_id=(row, turn + 1),
            device_id_type=MESH,
        )

    @pl.when(turn < batches - 1)
    def _():
        hist_copy().start()

    loads[0].wait()
    tap_row[...] = jnp.zeros_like(tap_row)
    tap_row[:, : taps.shape[1]] = taps[...].astype(F32) / 1024.0
    spread = jnp.broadcast_to(tap_row[...], (LANES, tap_row.shape[1]))
    rolled = pltpu.roll(spread, 0, 1, stride=1, stride_axis=0)
    wide = tap_row.shape[1]
    after = jnp.concatenate([rolled[:, wide - LANES :], rolled[:, :LANES]], axis=1)
    band = jnp.concatenate([rolled[:, LANES : 3 * LANES], rolled[:, : 2 * LANES], after], axis=0).astype(BF16)

    step = 2 * LANES
    loads[1].wait()
    for start in range(step, frame_count, step):
        filtered[:, start : start + step] = jnp.dot(
            frames[:, start - LANES : start + step], band, preferred_element_type=F32
        ).astype(BF16)
    here = jnp.dot(frames[:, :step], band[LANES:], preferred_element_type=F32)
    loads[2].wait()
    loads[3].wait()

    @pl.when(turn == 0)
    def _():
        history[...] = jnp.zeros_like(history)

    @pl.when(turn > 0)
    def _():
        hist_copy().wait_recv()

    filtered[:, :step] = (
        here + jnp.dot(history[...], band[:LANES], preferred_element_type=F32)
    ).astype(BF16)
    weighted[...] = jnp.dot(filtered[...], sketch[...], preferred_element_type=F32)

    @pl.when(turn > 0)
    def _():
        prev_copy().wait_recv()
        weighted[...] = rates[...] * before[...] + weighted[...]

    @pl.when(turn < batches - 1)
    def _():
        prev_copy().start()

    value = weighted[...]
    gram = jnp.dot(value.T, value, precision=HIGHEST, preferred_element_type=F32)
    half = rank // 2
    blocks = jnp.concatenate([gram[:half, :half], gram[:half, half:], gram[half:, half:]], axis=0)
    for index in range(count):
        parts[index] = cut(blocks, index, parts.shape[1], F32)
    gram_first = exchange(count, lambda peer: parts.at[peer], lambda mine: landed.at[mine], gram_a, gram_b)

    turned = filtered[...].T
    cross = jnp.zeros((frame_count, rank), F32)
    for piece in reversed(pieces(value)):
        cross = cross + jnp.dot(turned, piece.astype(BF16), preferred_element_type=F32)
    outer, inner = groups(count)
    plane, spot = place_of(count)
    shard = cross_total.shape[1]
    for index in range(count):
        cross_parts[index % inner, index // inner] = cut(cross, index, shard, F32)

    landed[row] = parts[row]
    total[row] = sum_slots(landed, gram_first)
    gram_across, gram_within = gather(count, total, gram_c, gram_d)
    ids = lax.broadcasted_iota(jnp.int32, (rank, rank), 0)
    cols = lax.broadcasted_iota(jnp.int32, (rank, rank), 1)
    work[:, rank:] = jnp.where(ids == cols, 1.0, 0.0).astype(F32)
    upper[...] = jnp.zeros_like(upper)
    inverse[...] = jnp.zeros_like(inverse)
    cross_landed[spot] = cross_parts[spot]
    for copy in gram_within:
        copy.wait_recv()
    cross_first = []
    for i in range(1, inner):
        other = lax.rem(spot + i, inner)
        cross_first.append(
            send(cross_parts.at[other], cross_landed.at[spot], cross_a, cross_b, i, plane * inner + other)
        )
    packed = jnp.concatenate([total[index] for index in range(count)], axis=0)
    across = packed[half:rank]
    work[:half, :half] = packed[:half]
    work[:half, half:rank] = across
    work[half:, :half] = across.T
    work[half:, half:rank] = packed[rank : rank + half]
    cross_second = []
    for begin in range(0, rank, LANES):
        eliminate(work, upper, inverse, begin)
        if begin == 0:
            cross_mid[...] = sum_slots(cross_landed, cross_first)
            cross_last[plane] = cross_mid[plane]
            for o in range(1, outer):
                other = lax.rem(plane + o, outer)
                cross_second.append(
                    send(cross_mid.at[other], cross_last.at[plane], cross_c, cross_d, o, other * inner + spot)
                )

    root = math.sqrt(npoints)
    against = (((1,), (1,)), ((), ()))
    mine = sum_slots(cross_last, cross_second) * (math.sqrt(rank) / root)
    cross_total[row] = lax.dot_general(
        mine, inverse[...], against, precision=HIGHEST, preferred_element_type=F32
    ).astype(BF16)
    cross_across, cross_within = gather(count, cross_total, cross_e, cross_f)
    factor[0] = jnp.where(cols >= ids, upper[...], 0.0) * (1.0 / root)
    store_factor = pltpu.make_async_copy(factor, factor_hbm, store_sems.at[0])
    store_factor.start()
    basis[0] = lax.dot_general(
        weighted[...], inverse[...], against, precision=HIGHEST, preferred_element_type=F32
    ) * root
    store_basis = pltpu.make_async_copy(basis, basis_hbm, store_sems.at[1])
    store_basis.start()
    for copy in cross_within:
        copy.wait_recv()
    for index in range(count):
        low = index * shard
        if low < frame_count:
            coeffs[low : low + shard] = cross_total[index]

    store_factor.wait()
    store_basis.wait()
    sent = gram_first + gram_across + gram_within + cross_first + cross_second + cross_across + cross_within
    for copy in sent:
        copy.wait_send()

    @pl.when(turn < batches - 1)
    def _():
        hist_copy().wait_send()
        prev_copy().wait_send()


def pieces(x):
    high = x.astype(BF16).astype(F32)
    rest = x - high
    mid = rest.astype(BF16).astype(F32)
    return high, mid, rest - mid


def eliminate(work, upper, inverse, begin):
    rank = work.shape[0]
    first = begin
    last = rank + begin + LANES
    width = rank - first
    tiles = PANEL // TILE
    full = (TILE, LANES)

    def wide(x, copies):
        return jnp.concatenate([x] * copies, axis=1)

    def panel(index, _):
        offset = pl.multiple_of(index * PANEL, PANEL)
        rows = pl.ds(pl.multiple_of(begin + offset, PANEL), PANEL)
        block = work[rows, first:last]
        corner = pltpu.roll(block[:, :LANES], lax.rem(LANES - offset, LANES), 1)
        block = jnp.concatenate([block, corner], axis=1)
        copies = block.shape[1] // LANES
        body = [block[b * TILE : (b + 1) * TILE] for b in range(tiles)]
        place = lax.broadcasted_iota(jnp.int32, body[0].shape, 0)
        for c in range(tiles):
            columns = [
                [
                    jnp.broadcast_to(body[b][:, at : at + 1], full)
                    for at in range(last - first + c * TILE, last - first + (c + 1) * TILE)
                ]
                for b in range(c, tiles)
            ]
            held = {
                (i, j): jnp.broadcast_to(columns[0][j][i : i + 1], full)
                for j in range(TILE)
                for i in range(j, TILE)
            }
            lines = [jnp.broadcast_to(body[c][i : i + 1], body[c].shape) for i in range(TILE)]
            result = jnp.zeros_like(body[c])
            for j in range(TILE):
                scale = lax.rsqrt(held[j, j])
                factors = {i: held[i, j] * scale for i in range(j + 1, TILE)}
                for i in range(j + 1, TILE):
                    for k in range(j + 1, i + 1):
                        held[i, k] = held[i, k] - factors[i] * factors[k]
                done = lines[j] * wide(scale, copies)
                for i in range(j + 1, TILE):
                    lines[i] = lines[i] - wide(factors[i], copies) * done
                for b in range(c + 1, tiles):
                    down = columns[b - c][j] * scale
                    for k in range(j + 1, TILE):
                        columns[b - c][k] = columns[b - c][k] - down * factors[k]
                    body[b] = body[b] - wide(down, copies) * done
                result = jnp.where(place == j, done, result)
            body[c] = result
        solved = jnp.concatenate(body, axis=0)[:, : last - first]
        upper[rows, first:rank] = solved[:, :width]
        inverse[rows, : begin + LANES] = solved[:, width:]
        high, mid, low = pieces(solved)
        left = jnp.concatenate([high, high, mid, high, mid, low], axis=0)[:, :width].astype(BF16)
        right = jnp.concatenate([high, mid, high, low, mid, high], axis=0).astype(BF16)
        work[first:, first:last] = work[first:, first:last] - lax.dot_general(
            left, right, (((0,), (0,)), ((), ())), preferred_element_type=F32
        )
        return 0

    lax.fori_loop(0, LANES // PANEL, panel, 0)


def finish_kernel(basis, factor, turned, basis_out, factor_out, coeffs_out, done):
    copies = [
        pltpu.make_async_copy(basis, basis_out, done.at[0]),
        pltpu.make_async_copy(factor, factor_out, done.at[1]),
    ]
    for copy in copies:
        copy.start()
    coeffs_out[0] = turned[...].astype(F32).T
    for copy in copies:
        copy.wait()


def shard_rows(length, count, tile):
    return tile * -(-length // (tile * count))


def shards(frames, tap_table, sketch_matrix, decay_rates):
    count, batches = lax.axis_size("rows"), lax.axis_size("batch")
    rows_here, frame_count = frames.shape
    rank = sketch_matrix.shape[1]
    half = rank // 2
    taps = tap_table.reshape(1, -1)
    gram_slots = pltpu.VMEM((count, shard_rows(3 * half, count, 8), half), F32)
    outer, inner = groups(count)
    shard = shard_rows(frame_count, count, 16)
    cross_slots = pltpu.VMEM((inner, outer, shard, rank), F32)
    cross_line = pltpu.VMEM((outer, shard, rank), F32)
    basis, factor, coeffs = pl.pallas_call(
        functools.partial(whole_kernel, count, batches, rows_here * count),
        out_shape=(
            jax.ShapeDtypeStruct((1, rows_here, rank), F32),
            jax.ShapeDtypeStruct((1, rank, rank), F32),
            jax.ShapeDtypeStruct((frame_count, rank), BF16),
        ),
        in_specs=[HBM_SPEC] * 4,
        out_specs=(HBM_SPEC, HBM_SPEC, VMEM_SPEC),
        scratch_shapes=[
            pltpu.VMEM(frames.shape, BF16),
            pltpu.VMEM(taps.shape, jnp.int32),
            pltpu.VMEM(sketch_matrix.shape, BF16),
            pltpu.VMEM(decay_rates.shape, F32),
            pltpu.VMEM((1, 4 * LANES), F32),
            pltpu.VMEM((rows_here, LANES), BF16),
            pltpu.VMEM((rows_here, rank), F32),
            pltpu.VMEM((rows_here, rank), F32),
            pltpu.VMEM((rows_here, frame_count), BF16),
            gram_slots,
            gram_slots,
            gram_slots,
            cross_slots,
            cross_slots,
            cross_line,
            cross_line,
            pltpu.VMEM((count, shard, rank), BF16),
            pltpu.VMEM((rank, 2 * rank), F32),
            pltpu.VMEM((rank, rank), F32),
            pltpu.VMEM((rank, rank), F32),
            pltpu.VMEM((1, rows_here, rank), F32),
            pltpu.VMEM((1, rank, rank), F32),
            pltpu.SemaphoreType.DMA((4,)),
            pltpu.SemaphoreType.DMA((2,)),
            pltpu.SemaphoreType.DMA((2,)),
            pltpu.SemaphoreType.DMA((2,)),
        ] + [pltpu.SemaphoreType.DMA((count,)) for _ in range(10)],
        compiler_params=pltpu.CompilerParams(
            collective_id=0, has_side_effects=True, vmem_limit_bytes=GRANT
        ),
        name="whole",
    )(frames, taps, sketch_matrix, decay_rates)
    return pl.pallas_call(
        finish_kernel,
        out_shape=(
            jax.ShapeDtypeStruct(basis.shape, F32),
            jax.ShapeDtypeStruct(factor.shape, F32),
            jax.ShapeDtypeStruct((1, rank, frame_count), F32),
        ),
        in_specs=[HBM_SPEC, HBM_SPEC, VMEM_SPEC],
        out_specs=(HBM_SPEC, HBM_SPEC, VMEM_SPEC),
        scratch_shapes=[pltpu.SemaphoreType.DMA((2,))],
        compiler_params=pltpu.CompilerParams(vmem_limit_bytes=GRANT),
        name="finish",
    )(basis, factor, coeffs)


def solution(mesh):
    placed = (P("rows", "batch"), P(), P(), P("batch", None))
    return jax.shard_map(
        shards,
        mesh=mesh,
        in_specs=placed,
        out_specs=(P("batch", "rows", None), P("batch", None, None), P("batch", None, None)),
        check_vma=False,
    )
```

```python
import functools
import math

import jax
import jax.numpy as jnp
from jax import lax
from jax.experimental import pallas as pl
from jax.experimental.pallas import tpu as pltpu
from jax.sharding import PartitionSpec as P

MESH = pl.DeviceIdType.MESH
HIGHEST = lax.Precision.HIGHEST
F32 = jnp.float32
BF16 = jnp.bfloat16
LANES = 128
PANEL = 32
TILE = 8
GRANT = 63 * 1024 * 1024
HBM_SPEC = pl.BlockSpec(memory_space=pltpu.HBM)
VMEM_SPEC = pl.BlockSpec(memory_space=pltpu.VMEM)


def greet(count, batches, with_batch):
    row, turn = lax.axis_index("rows"), lax.axis_index("batch")
    barrier = pltpu.get_barrier_semaphore()
    for step in range(1, count):
        pl.semaphore_signal(
            barrier, inc=1, device_id=(lax.rem(row + step, count), turn), device_id_type=MESH
        )
    waits = count - 1
    if with_batch and batches > 1:

        @pl.when(turn > 0)
        def _():
            pl.semaphore_signal(barrier, inc=1, device_id=(row, turn - 1), device_id_type=MESH)

        @pl.when(turn < batches - 1)
        def _():
            pl.semaphore_signal(barrier, inc=1, device_id=(row, turn + 1), device_id_type=MESH)

        waits = waits + jnp.where(turn > 0, 1, 0) + jnp.where(turn < batches - 1, 1, 0)
    pl.semaphore_wait(barrier, waits)


def exchange(count, source_of, target_of, send_sems, recv_sems):
    row, turn = lax.axis_index("rows"), lax.axis_index("batch")
    copies = []
    for step in range(1, count):
        peer = lax.rem(row + step, count)
        copy = pltpu.make_async_remote_copy(
            src_ref=source_of(peer),
            dst_ref=target_of(row),
            send_sem=send_sems.at[step],
            recv_sem=recv_sems.at[step],
            device_id=(peer, turn),
            device_id_type=MESH,
        )
        copy.start()
        copies.append(copy)
    return copies


def groups(count):
    inner = 4 if count % 4 == 0 else 1
    return count // inner, inner


def send(source, target, send_sems, recv_sems, index, peer):
    copy = pltpu.make_async_remote_copy(
        src_ref=source,
        dst_ref=target,
        send_sem=send_sems.at[index],
        recv_sem=recv_sems.at[index],
        device_id=(peer, lax.axis_index("batch")),
        device_id_type=MESH,
    )
    copy.start()
    return copy


def place_of(count):
    inner = groups(count)[1]
    row = lax.axis_index("rows")
    return lax.div(row, inner), lax.rem(row, inner)


def gather(count, total, send_sems, recv_sems):
    outer, inner = groups(count)
    plane, spot = place_of(count)
    row = lax.axis_index("rows")
    across, within = [], []
    for o in range(1, outer):
        peer = lax.rem(plane + o, outer) * inner + spot
        across.append(send(total.at[row], total.at[row], send_sems, recv_sems, o * inner, peer))
    for o in range(outer):
        if o > 0:
            across[o - 1].wait_recv()
        owner = lax.rem(plane - o + outer, outer) * inner + spot
        for i in range(1, inner):
            peer = plane * inner + lax.rem(spot + i, inner)
            within.append(send(total.at[owner], total.at[owner], send_sems, recv_sems, o * inner + i, peer))
    return across, within


def cut(value, index, shard, dtype):
    low = index * shard
    if low < value.shape[0]:
        return value[low : low + shard]
    return jnp.zeros((shard, value.shape[1]), dtype)


def sum_slots(landed, copies):
    for copy in copies:
        copy.wait_recv()
    summed = landed[0]
    for sender in range(1, landed.shape[0]):
        summed = summed + landed[sender]
    return summed


def whole_kernel(
    count, batches, npoints,
    frames_hbm, taps_hbm, sketch_hbm, rates_hbm, basis_hbm, factor_hbm, coeffs,
    frames, taps, sketch, rates, tap_row, history, before, weighted, filtered,
    parts, landed, total, cross_parts, cross_landed, cross_mid, cross_last, cross_total, work, upper, inverse, basis, factor,
    load_sems, store_sems, hist_sems, prev_sems, gram_a, gram_b, gram_c, gram_d, cross_a, cross_b, cross_c, cross_d, cross_e, cross_f,
):
    row, turn = lax.axis_index("rows"), lax.axis_index("batch")
    frame_count = frames.shape[1]
    rank = sketch.shape[1]
    loads = [
        pltpu.make_async_copy(source, target, load_sems.at[index])
        for index, (source, target) in enumerate(
            ((taps_hbm, taps), (frames_hbm, frames), (sketch_hbm, sketch), (rates_hbm, rates))
        )
    ]
    for load in loads:
        load.start()
    greet(count, batches, True)

    def hist_copy():
        return pltpu.make_async_remote_copy(
            src_ref=frames_hbm.at[:, pl.ds(frame_count - LANES, LANES)],
            dst_ref=history,
            send_sem=hist_sems.at[0],
            recv_sem=hist_sems.at[1],
            device_id=(row, turn + 1),
            device_id_type=MESH,
        )

    def prev_copy():
        return pltpu.make_async_remote_copy(
            src_ref=weighted,
            dst_ref=before,
            send_sem=prev_sems.at[0],
            recv_sem=prev_sems.at[1],
            device_id=(row, turn + 1),
            device_id_type=MESH,
        )

    @pl.when(turn < batches - 1)
    def _():
        hist_copy().start()

    loads[0].wait()
    tap_row[...] = jnp.zeros_like(tap_row)
    tap_row[:, : taps.shape[1]] = taps[...].astype(F32) / 1024.0
    spread = jnp.broadcast_to(tap_row[...], (LANES, tap_row.shape[1]))
    rolled = pltpu.roll(spread, 0, 1, stride=1, stride_axis=0)
    wide = tap_row.shape[1]
    after = jnp.concatenate([rolled[:, wide - LANES :], rolled[:, :LANES]], axis=1)
    band = jnp.concatenate([rolled[:, LANES : 3 * LANES], rolled[:, : 2 * LANES], after], axis=0).astype(BF16)

    step = 2 * LANES
    loads[1].wait()
    for start in range(step, frame_count, step):
        filtered[:, start : start + step] = jnp.dot(
            frames[:, start - LANES : start + step], band, preferred_element_type=F32
        ).astype(BF16)
    here = jnp.dot(frames[:, :step], band[LANES:], preferred_element_type=F32)
    loads[2].wait()
    loads[3].wait()

    @pl.when(turn == 0)
    def _():
        history[...] = jnp.zeros_like(history)

    @pl.when(turn > 0)
    def _():
        hist_copy().wait_recv()

    filtered[:, :step] = (
        here + jnp.dot(history[...], band[:LANES], preferred_element_type=F32)
    ).astype(BF16)
    weighted[...] = jnp.dot(filtered[...], sketch[...], preferred_element_type=F32)

    @pl.when(turn > 0)
    def _():
        prev_copy().wait_recv()
        weighted[...] = rates[...] * before[...] + weighted[...]

    @pl.when(turn < batches - 1)
    def _():
        prev_copy().start()

    value = weighted[...]
    gram = jnp.dot(value.T, value, precision=HIGHEST, preferred_element_type=F32)
    half = rank // 2
    blocks = jnp.concatenate([gram[:half, :half], gram[:half, half:], gram[half:, half:]], axis=0)
    for index in range(count):
        parts[index] = cut(blocks, index, parts.shape[1], F32)
    gram_first = exchange(count, lambda peer: parts.at[peer], lambda mine: landed.at[mine], gram_a, gram_b)

    turned = filtered[...].T
    cross = jnp.zeros((frame_count, rank), F32)
    for piece in reversed(pieces(value)):
        cross = cross + jnp.dot(turned, piece.astype(BF16), preferred_element_type=F32)
    outer, inner = groups(count)
    plane, spot = place_of(count)
    shard = cross_total.shape[1]
    for index in range(count):
        cross_parts[index % inner, index // inner] = cut(cross, index, shard, F32)
    cross_first = []
    for i in range(1, inner):
        other = lax.rem(spot + i, inner)
        cross_first.append(
            send(cross_parts.at[other], cross_landed.at[spot], cross_a, cross_b, i, plane * inner + other)
        )
    cross_landed[spot] = cross_parts[spot]

    landed[row] = parts[row]
    total[row] = sum_slots(landed, gram_first)
    gram_across, gram_within = gather(count, total, gram_c, gram_d)
    ids = lax.broadcasted_iota(jnp.int32, (rank, rank), 0)
    cols = lax.broadcasted_iota(jnp.int32, (rank, rank), 1)
    work[:, rank:] = jnp.where(ids == cols, 1.0, 0.0).astype(F32)
    upper[...] = jnp.zeros_like(upper)
    inverse[...] = jnp.zeros_like(inverse)
    for copy in gram_within:
        copy.wait_recv()
    cross_mid[...] = sum_slots(cross_landed, cross_first)
    cross_last[plane] = cross_mid[plane]
    cross_second = []
    for o in range(1, outer):
        other = lax.rem(plane + o, outer)
        cross_second.append(
            send(cross_mid.at[other], cross_last.at[plane], cross_c, cross_d, o, other * inner + spot)
        )
    packed = jnp.concatenate([total[index] for index in range(count)], axis=0)
    across = packed[half:rank]
    work[:half, :half] = packed[:half]
    work[:half, half:rank] = across
    work[half:, :half] = across.T
    work[half:, half:rank] = packed[rank : rank + half]
    for begin in range(0, rank, LANES):
        eliminate(work, upper, inverse, begin)

    root = math.sqrt(npoints)
    against = (((1,), (1,)), ((), ()))
    mine = sum_slots(cross_last, cross_second) * (math.sqrt(rank) / root)
    cross_total[row] = lax.dot_general(
        mine, inverse[...], against, precision=HIGHEST, preferred_element_type=F32
    ).astype(BF16)
    cross_across, cross_within = gather(count, cross_total, cross_e, cross_f)
    factor[0] = jnp.where(cols >= ids, upper[...], 0.0) * (1.0 / root)
    store_factor = pltpu.make_async_copy(factor, factor_hbm, store_sems.at[0])
    store_factor.start()
    basis[0] = lax.dot_general(
        weighted[...], inverse[...], against, precision=HIGHEST, preferred_element_type=F32
    ) * root
    store_basis = pltpu.make_async_copy(basis, basis_hbm, store_sems.at[1])
    store_basis.start()
    for copy in cross_within:
        copy.wait_recv()
    for index in range(count):
        low = index * shard
        if low < frame_count:
            coeffs[low : low + shard] = cross_total[index]

    store_factor.wait()
    store_basis.wait()
    sent = gram_first + gram_across + gram_within + cross_first + cross_second + cross_across + cross_within
    for copy in sent:
        copy.wait_send()

    @pl.when(turn < batches - 1)
    def _():
        hist_copy().wait_send()
        prev_copy().wait_send()


def pieces(x):
    high = x.astype(BF16).astype(F32)
    rest = x - high
    mid = rest.astype(BF16).astype(F32)
    return high, mid, rest - mid


def eliminate(work, upper, inverse, begin):
    rank = work.shape[0]
    first = begin
    last = rank + begin + LANES
    width = rank - first
    tiles = PANEL // TILE
    full = (TILE, LANES)

    def wide(x, copies):
        return jnp.concatenate([x] * copies, axis=1)

    def panel(index, _):
        offset = pl.multiple_of(index * PANEL, PANEL)
        rows = pl.ds(pl.multiple_of(begin + offset, PANEL), PANEL)
        block = work[rows, first:last]
        corner = pltpu.roll(block[:, :LANES], lax.rem(LANES - offset, LANES), 1)
        block = jnp.concatenate([block, corner], axis=1)
        copies = block.shape[1] // LANES
        body = [block[b * TILE : (b + 1) * TILE] for b in range(tiles)]
        place = lax.broadcasted_iota(jnp.int32, body[0].shape, 0)
        for c in range(tiles):
            columns = [
                [
                    jnp.broadcast_to(body[b][:, at : at + 1], full)
                    for at in range(last - first + c * TILE, last - first + (c + 1) * TILE)
                ]
                for b in range(c, tiles)
            ]
            held = {
                (i, j): jnp.broadcast_to(columns[0][j][i : i + 1], full)
                for j in range(TILE)
                for i in range(j, TILE)
            }
            lines = [jnp.broadcast_to(body[c][i : i + 1], body[c].shape) for i in range(TILE)]
            result = jnp.zeros_like(body[c])
            for j in range(TILE):
                scale = lax.rsqrt(held[j, j])
                factors = {i: held[i, j] * scale for i in range(j + 1, TILE)}
                for i in range(j + 1, TILE):
                    for k in range(j + 1, i + 1):
                        held[i, k] = held[i, k] - factors[i] * factors[k]
                done = lines[j] * wide(scale, copies)
                for i in range(j + 1, TILE):
                    lines[i] = lines[i] - wide(factors[i], copies) * done
                for b in range(c + 1, tiles):
                    down = columns[b - c][j] * scale
                    for k in range(j + 1, TILE):
                        columns[b - c][k] = columns[b - c][k] - down * factors[k]
                    body[b] = body[b] - wide(down, copies) * done
                result = jnp.where(place == j, done, result)
            body[c] = result
        solved = jnp.concatenate(body, axis=0)[:, : last - first]
        upper[rows, first:rank] = solved[:, :width]
        inverse[rows, : begin + LANES] = solved[:, width:]
        high, mid, low = pieces(solved)
        left = jnp.concatenate([high, high, mid, high, mid, low], axis=0)[:, :width].astype(BF16)
        right = jnp.concatenate([high, mid, high, low, mid, high], axis=0).astype(BF16)
        work[first:, first:last] = work[first:, first:last] - lax.dot_general(
            left, right, (((0,), (0,)), ((), ())), preferred_element_type=F32
        )
        return 0

    lax.fori_loop(0, LANES // PANEL, panel, 0)


def finish_kernel(
    basis_in, factor_in, turned_in, basis_out, factor_out, coeffs_out, basis, factor, turned, coeffs, loaded, stored
):
    loads = [
        pltpu.make_async_copy(source, target, loaded.at[index])
        for index, (source, target) in enumerate(((turned_in, turned), (basis_in, basis), (factor_in, factor)))
    ]
    stores = [
        pltpu.make_async_copy(source, target, stored.at[index])
        for index, (source, target) in enumerate(((coeffs, coeffs_out), (basis, basis_out), (factor, factor_out)))
    ]
    for load in loads:
        load.start()
    for index in (1, 2):
        loads[index].wait()
        stores[index].start()
    loads[0].wait()
    coeffs[0] = turned[...].astype(F32).T
    stores[0].start()
    for store in stores:
        store.wait()


def shard_rows(length, count, tile):
    return tile * -(-length // (tile * count))


def shards(frames, tap_table, sketch_matrix, decay_rates):
    count, batches = lax.axis_size("rows"), lax.axis_size("batch")
    rows_here, frame_count = frames.shape
    rank = sketch_matrix.shape[1]
    half = rank // 2
    taps = tap_table.reshape(1, -1)
    gram_slots = pltpu.VMEM((count, shard_rows(3 * half, count, 8), half), F32)
    outer, inner = groups(count)
    shard = shard_rows(frame_count, count, 16)
    cross_slots = pltpu.VMEM((inner, outer, shard, rank), F32)
    cross_line = pltpu.VMEM((outer, shard, rank), F32)
    basis, factor, coeffs = pl.pallas_call(
        functools.partial(whole_kernel, count, batches, rows_here * count),
        out_shape=(
            jax.ShapeDtypeStruct((1, rows_here, rank), F32),
            jax.ShapeDtypeStruct((1, rank, rank), F32),
            jax.ShapeDtypeStruct((frame_count, rank), BF16),
        ),
        in_specs=[HBM_SPEC] * 4,
        out_specs=(HBM_SPEC, HBM_SPEC, VMEM_SPEC),
        scratch_shapes=[
            pltpu.VMEM(frames.shape, BF16),
            pltpu.VMEM(taps.shape, jnp.int32),
            pltpu.VMEM(sketch_matrix.shape, BF16),
            pltpu.VMEM(decay_rates.shape, F32),
            pltpu.VMEM((1, 4 * LANES), F32),
            pltpu.VMEM((rows_here, LANES), BF16),
            pltpu.VMEM((rows_here, rank), F32),
            pltpu.VMEM((rows_here, rank), F32),
            pltpu.VMEM((rows_here, frame_count), BF16),
            gram_slots,
            gram_slots,
            gram_slots,
            cross_slots,
            cross_slots,
            cross_line,
            cross_line,
            pltpu.VMEM((count, shard, rank), BF16),
            pltpu.VMEM((rank, 2 * rank), F32),
            pltpu.VMEM((rank, rank), F32),
            pltpu.VMEM((rank, rank), F32),
            pltpu.VMEM((1, rows_here, rank), F32),
            pltpu.VMEM((1, rank, rank), F32),
            pltpu.SemaphoreType.DMA((4,)),
            pltpu.SemaphoreType.DMA((2,)),
            pltpu.SemaphoreType.DMA((2,)),
            pltpu.SemaphoreType.DMA((2,)),
        ] + [pltpu.SemaphoreType.DMA((count,)) for _ in range(10)],
        compiler_params=pltpu.CompilerParams(
            collective_id=0, has_side_effects=True, vmem_limit_bytes=GRANT
        ),
        name="whole",
    )(frames, taps, sketch_matrix, decay_rates)
    return pl.pallas_call(
        finish_kernel,
        out_shape=(
            jax.ShapeDtypeStruct(basis.shape, F32),
            jax.ShapeDtypeStruct(factor.shape, F32),
            jax.ShapeDtypeStruct((1, rank, frame_count), F32),
        ),
        in_specs=[HBM_SPEC] * 3,
        out_specs=(HBM_SPEC,) * 3,
        scratch_shapes=[
            pltpu.VMEM(basis.shape, F32),
            pltpu.VMEM(factor.shape, F32),
            pltpu.VMEM(coeffs.shape, BF16),
            pltpu.VMEM((1, rank, frame_count), F32),
            pltpu.SemaphoreType.DMA((3,)),
            pltpu.SemaphoreType.DMA((3,)),
        ],
        compiler_params=pltpu.CompilerParams(vmem_limit_bytes=GRANT),
        name="finish",
    )(basis, factor, coeffs)


def solution(mesh):
    placed = (P("rows", "batch"), P(), P(), P("batch", None))
    return jax.shard_map(
        shards,
        mesh=mesh,
        in_specs=placed,
        out_specs=(P("batch", "rows", None), P("batch", None, None), P("batch", None, None)),
        check_vma=False,
    )
```

```python
import functools
import math

import jax
import jax.numpy as jnp
from jax import lax
from jax.experimental import pallas as pl
from jax.experimental.pallas import tpu as pltpu
from jax.sharding import PartitionSpec as P

MESH = pl.DeviceIdType.MESH
HIGHEST = lax.Precision.HIGHEST
F32 = jnp.float32
BF16 = jnp.bfloat16
LANES = 128
PANEL = 32
TILE = 8
GRANT = 63 * 1024 * 1024
HBM_SPEC = pl.BlockSpec(memory_space=pltpu.HBM)
VMEM_SPEC = pl.BlockSpec(memory_space=pltpu.VMEM)


def greet(count, batches, with_batch):
    row, turn = lax.axis_index("rows"), lax.axis_index("batch")
    barrier = pltpu.get_barrier_semaphore()
    for step in range(1, count):
        pl.semaphore_signal(
            barrier, inc=1, device_id=(lax.rem(row + step, count), turn), device_id_type=MESH
        )
    waits = count - 1
    if with_batch and batches > 1:

        @pl.when(turn > 0)
        def _():
            pl.semaphore_signal(barrier, inc=1, device_id=(row, turn - 1), device_id_type=MESH)

        @pl.when(turn < batches - 1)
        def _():
            pl.semaphore_signal(barrier, inc=1, device_id=(row, turn + 1), device_id_type=MESH)

        waits = waits + jnp.where(turn > 0, 1, 0) + jnp.where(turn < batches - 1, 1, 0)
    pl.semaphore_wait(barrier, waits)


def exchange(count, source_of, target_of, send_sems, recv_sems):
    row, turn = lax.axis_index("rows"), lax.axis_index("batch")
    copies = []
    for step in range(1, count):
        peer = lax.rem(row + step, count)
        copy = pltpu.make_async_remote_copy(
            src_ref=source_of(peer),
            dst_ref=target_of(row),
            send_sem=send_sems.at[step],
            recv_sem=recv_sems.at[step],
            device_id=(peer, turn),
            device_id_type=MESH,
        )
        copy.start()
        copies.append(copy)
    return copies


def groups(count):
    inner = 4 if count % 4 == 0 else 1
    return count // inner, inner


def send(source, target, send_sems, recv_sems, index, peer):
    copy = pltpu.make_async_remote_copy(
        src_ref=source,
        dst_ref=target,
        send_sem=send_sems.at[index],
        recv_sem=recv_sems.at[index],
        device_id=(peer, lax.axis_index("batch")),
        device_id_type=MESH,
    )
    copy.start()
    return copy


def place_of(count):
    inner = groups(count)[1]
    row = lax.axis_index("rows")
    return lax.div(row, inner), lax.rem(row, inner)


def gather(count, total, send_sems, recv_sems):
    outer, inner = groups(count)
    plane, spot = place_of(count)
    row = lax.axis_index("rows")
    across, within = [], []
    for o in range(1, outer):
        peer = lax.rem(plane + o, outer) * inner + spot
        across.append(send(total.at[row], total.at[row], send_sems, recv_sems, o * inner, peer))
    for o in range(outer):
        if o > 0:
            across[o - 1].wait_recv()
        owner = lax.rem(plane - o + outer, outer) * inner + spot
        for i in range(1, inner):
            peer = plane * inner + lax.rem(spot + i, inner)
            within.append(send(total.at[owner], total.at[owner], send_sems, recv_sems, o * inner + i, peer))
    return across, within


def cut(value, index, shard, dtype):
    low = index * shard
    if low < value.shape[0]:
        return value[low : low + shard]
    return jnp.zeros((shard, value.shape[1]), dtype)


def sum_slots(landed, copies):
    for copy in copies:
        copy.wait_recv()
    summed = landed[0]
    for sender in range(1, landed.shape[0]):
        summed = summed + landed[sender]
    return summed


def whole_kernel(
    count, batches, npoints,
    frames_hbm, taps_hbm, sketch_hbm, rates_hbm, basis_hbm, factor_hbm, coeffs,
    frames, taps, sketch, rates, tap_row, history, before, weighted, filtered,
    parts, landed, total, late_parts, late_landed, late_total, cross_parts, cross_landed, cross_mid, cross_last, cross_total, work, upper, inverse, basis, factor,
    load_sems, store_sems, hist_sems, prev_sems, gram_a, gram_b, gram_c, gram_d, late_a, late_b, late_c, late_d, cross_a, cross_b, cross_c, cross_d, cross_e, cross_f,
):
    row, turn = lax.axis_index("rows"), lax.axis_index("batch")
    frame_count = frames.shape[1]
    rank = sketch.shape[1]
    loads = [
        pltpu.make_async_copy(source, target, load_sems.at[index])
        for index, (source, target) in enumerate(
            ((taps_hbm, taps), (frames_hbm, frames), (sketch_hbm, sketch), (rates_hbm, rates))
        )
    ]
    for load in loads:
        load.start()
    greet(count, batches, True)

    def hist_copy():
        return pltpu.make_async_remote_copy(
            src_ref=frames_hbm.at[:, pl.ds(frame_count - LANES, LANES)],
            dst_ref=history,
            send_sem=hist_sems.at[0],
            recv_sem=hist_sems.at[1],
            device_id=(row, turn + 1),
            device_id_type=MESH,
        )

    def prev_copy():
        return pltpu.make_async_remote_copy(
            src_ref=weighted,
            dst_ref=before,
            send_sem=prev_sems.at[0],
            recv_sem=prev_sems.at[1],
            device_id=(row, turn + 1),
            device_id_type=MESH,
        )

    @pl.when(turn < batches - 1)
    def _():
        hist_copy().start()

    loads[0].wait()
    tap_row[...] = jnp.zeros_like(tap_row)
    tap_row[:, : taps.shape[1]] = taps[...].astype(F32) / 1024.0
    spread = jnp.broadcast_to(tap_row[...], (LANES, tap_row.shape[1]))
    rolled = pltpu.roll(spread, 0, 1, stride=1, stride_axis=0)
    wide = tap_row.shape[1]
    after = jnp.concatenate([rolled[:, wide - LANES :], rolled[:, :LANES]], axis=1)
    band = jnp.concatenate([rolled[:, LANES : 3 * LANES], rolled[:, : 2 * LANES], after], axis=0).astype(BF16)

    step = 2 * LANES
    loads[1].wait()
    for start in range(step, frame_count, step):
        filtered[:, start : start + step] = jnp.dot(
            frames[:, start - LANES : start + step], band, preferred_element_type=F32
        ).astype(BF16)
    here = jnp.dot(frames[:, :step], band[LANES:], preferred_element_type=F32)
    loads[2].wait()
    loads[3].wait()

    @pl.when(turn == 0)
    def _():
        history[...] = jnp.zeros_like(history)

    @pl.when(turn > 0)
    def _():
        hist_copy().wait_recv()

    filtered[:, :step] = (
        here + jnp.dot(history[...], band[:LANES], preferred_element_type=F32)
    ).astype(BF16)
    weighted[...] = jnp.dot(filtered[...], sketch[...], preferred_element_type=F32)

    @pl.when(turn > 0)
    def _():
        prev_copy().wait_recv()
        weighted[...] = rates[...] * before[...] + weighted[...]

    @pl.when(turn < batches - 1)
    def _():
        prev_copy().start()

    value = weighted[...]
    gram = jnp.dot(value.T, value, precision=HIGHEST, preferred_element_type=F32)
    half = rank // 2
    blocks = jnp.concatenate([gram[:half, :half], gram[:half, half:]], axis=0)
    corner = gram[half:, half:]
    for index in range(count):
        parts[index] = cut(blocks, index, parts.shape[1], F32)
    gram_first = exchange(count, lambda peer: parts.at[peer], lambda mine: landed.at[mine], gram_a, gram_b)
    for index in range(count):
        late_parts[index] = cut(corner, index, late_parts.shape[1], F32)
    late_first = exchange(
        count, lambda peer: late_parts.at[peer], lambda mine: late_landed.at[mine], late_a, late_b
    )

    turned = filtered[...].T
    cross = jnp.zeros((frame_count, rank), F32)
    for piece in reversed(pieces(value)):
        cross = cross + jnp.dot(turned, piece.astype(BF16), preferred_element_type=F32)
    outer, inner = groups(count)
    plane, spot = place_of(count)
    shard = cross_total.shape[1]
    for index in range(count):
        cross_parts[index % inner, index // inner] = cut(cross, index, shard, F32)
    cross_first = []
    for i in range(1, inner):
        other = lax.rem(spot + i, inner)
        cross_first.append(
            send(cross_parts.at[other], cross_landed.at[spot], cross_a, cross_b, i, plane * inner + other)
        )
    cross_landed[spot] = cross_parts[spot]

    landed[row] = parts[row]
    total[row] = sum_slots(landed, gram_first)
    gram_across, gram_within = gather(count, total, gram_c, gram_d)
    late_landed[row] = late_parts[row]
    late_total[row] = sum_slots(late_landed, late_first)
    late_second = exchange(
        count, lambda peer: late_total.at[row], lambda mine: late_total.at[mine], late_c, late_d
    )
    ids = lax.broadcasted_iota(jnp.int32, (rank, rank), 0)
    cols = lax.broadcasted_iota(jnp.int32, (rank, rank), 1)
    work[:, rank:] = jnp.where(ids == cols, 1.0, 0.0).astype(F32)
    upper[...] = jnp.zeros_like(upper)
    inverse[...] = jnp.zeros_like(inverse)
    for copy in gram_within:
        copy.wait_recv()
    cross_mid[...] = sum_slots(cross_landed, cross_first)
    cross_last[plane] = cross_mid[plane]
    cross_second = []
    for o in range(1, outer):
        other = lax.rem(plane + o, outer)
        cross_second.append(
            send(cross_mid.at[other], cross_last.at[plane], cross_c, cross_d, o, other * inner + spot)
        )
    packed = jnp.concatenate([total[index] for index in range(count)], axis=0)
    across = packed[half:rank]
    work[:half, :half] = packed[:half]
    work[:half, half:rank] = across
    work[half:, :half] = across.T
    work[half:, half:rank] = jnp.zeros((half, half), F32)
    eliminate(work, upper, inverse, 0)
    for copy in late_second:
        copy.wait_recv()
    corner = jnp.concatenate([late_total[index] for index in range(count)], axis=0)
    work[half:, half:rank] = work[half:, half:rank] + corner[:half]
    eliminate(work, upper, inverse, half)

    root = math.sqrt(npoints)
    against = (((1,), (1,)), ((), ()))
    mine = sum_slots(cross_last, cross_second) * (math.sqrt(rank) / root)
    cross_total[row] = lax.dot_general(
        mine, inverse[...], against, precision=HIGHEST, preferred_element_type=F32
    ).astype(BF16)
    cross_across, cross_within = gather(count, cross_total, cross_e, cross_f)
    factor[0] = jnp.where(cols >= ids, upper[...], 0.0) * (1.0 / root)
    store_factor = pltpu.make_async_copy(factor, factor_hbm, store_sems.at[0])
    store_factor.start()
    basis[0] = lax.dot_general(
        weighted[...], inverse[...], against, precision=HIGHEST, preferred_element_type=F32
    ) * root
    store_basis = pltpu.make_async_copy(basis, basis_hbm, store_sems.at[1])
    store_basis.start()
    for copy in cross_within:
        copy.wait_recv()
    for index in range(count):
        low = index * shard
        if low < frame_count:
            coeffs[low : low + shard] = cross_total[index]

    store_factor.wait()
    store_basis.wait()
    sent = late_first + late_second + gram_first + gram_across + gram_within + cross_first + cross_second + cross_across + cross_within
    for copy in sent:
        copy.wait_send()

    @pl.when(turn < batches - 1)
    def _():
        hist_copy().wait_send()
        prev_copy().wait_send()


def pieces(x):
    high = x.astype(BF16).astype(F32)
    rest = x - high
    mid = rest.astype(BF16).astype(F32)
    return high, mid, rest - mid


def eliminate(work, upper, inverse, begin):
    rank = work.shape[0]
    first = begin
    last = rank + begin + LANES
    width = rank - first
    tiles = PANEL // TILE
    full = (TILE, LANES)

    def wide(x, copies):
        return jnp.concatenate([x] * copies, axis=1)

    def panel(index, _):
        offset = pl.multiple_of(index * PANEL, PANEL)
        rows = pl.ds(pl.multiple_of(begin + offset, PANEL), PANEL)
        block = work[rows, first:last]
        corner = pltpu.roll(block[:, :LANES], lax.rem(LANES - offset, LANES), 1)
        block = jnp.concatenate([block, corner], axis=1)
        copies = block.shape[1] // LANES
        body = [block[b * TILE : (b + 1) * TILE] for b in range(tiles)]
        place = lax.broadcasted_iota(jnp.int32, body[0].shape, 0)
        for c in range(tiles):
            columns = [
                [
                    jnp.broadcast_to(body[b][:, at : at + 1], full)
                    for at in range(last - first + c * TILE, last - first + (c + 1) * TILE)
                ]
                for b in range(c, tiles)
            ]
            held = {
                (i, j): jnp.broadcast_to(columns[0][j][i : i + 1], full)
                for j in range(TILE)
                for i in range(j, TILE)
            }
            lines = [jnp.broadcast_to(body[c][i : i + 1], body[c].shape) for i in range(TILE)]
            result = jnp.zeros_like(body[c])
            for j in range(TILE):
                scale = lax.rsqrt(held[j, j])
                factors = {i: held[i, j] * scale for i in range(j + 1, TILE)}
                for i in range(j + 1, TILE):
                    for k in range(j + 1, i + 1):
                        held[i, k] = held[i, k] - factors[i] * factors[k]
                done = lines[j] * wide(scale, copies)
                for i in range(j + 1, TILE):
                    lines[i] = lines[i] - wide(factors[i], copies) * done
                for b in range(c + 1, tiles):
                    down = columns[b - c][j] * scale
                    for k in range(j + 1, TILE):
                        columns[b - c][k] = columns[b - c][k] - down * factors[k]
                    body[b] = body[b] - wide(down, copies) * done
                result = jnp.where(place == j, done, result)
            body[c] = result
        solved = jnp.concatenate(body, axis=0)[:, : last - first]
        upper[rows, first:rank] = solved[:, :width]
        inverse[rows, : begin + LANES] = solved[:, width:]
        high, mid, low = pieces(solved)
        left = jnp.concatenate([high, high, mid, high, mid, low], axis=0)[:, :width].astype(BF16)
        right = jnp.concatenate([high, mid, high, low, mid, high], axis=0).astype(BF16)
        work[first:, first:last] = work[first:, first:last] - lax.dot_general(
            left, right, (((0,), (0,)), ((), ())), preferred_element_type=F32
        )
        return 0

    lax.fori_loop(0, LANES // PANEL, panel, 0)


def finish_kernel(
    basis_in, factor_in, turned_in, basis_out, factor_out, coeffs_out, basis, factor, turned, coeffs, loaded, stored
):
    loads = [
        pltpu.make_async_copy(source, target, loaded.at[index])
        for index, (source, target) in enumerate(((turned_in, turned), (basis_in, basis), (factor_in, factor)))
    ]
    stores = [
        pltpu.make_async_copy(source, target, stored.at[index])
        for index, (source, target) in enumerate(((coeffs, coeffs_out), (basis, basis_out), (factor, factor_out)))
    ]
    for load in loads:
        load.start()
    for index in (1, 2):
        loads[index].wait()
        stores[index].start()
    loads[0].wait()
    coeffs[0] = turned[...].astype(F32).T
    stores[0].start()
    for store in stores:
        store.wait()


def shard_rows(length, count, tile):
    return tile * -(-length // (tile * count))


def shards(frames, tap_table, sketch_matrix, decay_rates):
    count, batches = lax.axis_size("rows"), lax.axis_size("batch")
    rows_here, frame_count = frames.shape
    rank = sketch_matrix.shape[1]
    half = rank // 2
    taps = tap_table.reshape(1, -1)
    gram_slots = pltpu.VMEM((count, shard_rows(2 * half, count, 8), half), F32)
    late_slots = pltpu.VMEM((count, shard_rows(half, count, 8), half), F32)
    outer, inner = groups(count)
    shard = shard_rows(frame_count, count, 16)
    cross_slots = pltpu.VMEM((inner, outer, shard, rank), F32)
    cross_line = pltpu.VMEM((outer, shard, rank), F32)
    basis, factor, coeffs = pl.pallas_call(
        functools.partial(whole_kernel, count, batches, rows_here * count),
        out_shape=(
            jax.ShapeDtypeStruct((1, rows_here, rank), F32),
            jax.ShapeDtypeStruct((1, rank, rank), F32),
            jax.ShapeDtypeStruct((frame_count, rank), BF16),
        ),
        in_specs=[HBM_SPEC] * 4,
        out_specs=(HBM_SPEC, HBM_SPEC, VMEM_SPEC),
        scratch_shapes=[
            pltpu.VMEM(frames.shape, BF16),
            pltpu.VMEM(taps.shape, jnp.int32),
            pltpu.VMEM(sketch_matrix.shape, BF16),
            pltpu.VMEM(decay_rates.shape, F32),
            pltpu.VMEM((1, 4 * LANES), F32),
            pltpu.VMEM((rows_here, LANES), BF16),
            pltpu.VMEM((rows_here, rank), F32),
            pltpu.VMEM((rows_here, rank), F32),
            pltpu.VMEM((rows_here, frame_count), BF16),
            gram_slots,
            gram_slots,
            gram_slots,
            late_slots,
            late_slots,
            late_slots,
            cross_slots,
            cross_slots,
            cross_line,
            cross_line,
            pltpu.VMEM((count, shard, rank), BF16),
            pltpu.VMEM((rank, 2 * rank), F32),
            pltpu.VMEM((rank, rank), F32),
            pltpu.VMEM((rank, rank), F32),
            pltpu.VMEM((1, rows_here, rank), F32),
            pltpu.VMEM((1, rank, rank), F32),
            pltpu.SemaphoreType.DMA((4,)),
            pltpu.SemaphoreType.DMA((2,)),
            pltpu.SemaphoreType.DMA((2,)),
            pltpu.SemaphoreType.DMA((2,)),
        ] + [pltpu.SemaphoreType.DMA((count,)) for _ in range(14)],
        compiler_params=pltpu.CompilerParams(
            collective_id=0, has_side_effects=True, vmem_limit_bytes=GRANT
        ),
        name="whole",
    )(frames, taps, sketch_matrix, decay_rates)
    return pl.pallas_call(
        finish_kernel,
        out_shape=(
            jax.ShapeDtypeStruct(basis.shape, F32),
            jax.ShapeDtypeStruct(factor.shape, F32),
            jax.ShapeDtypeStruct((1, rank, frame_count), F32),
        ),
        in_specs=[HBM_SPEC] * 3,
        out_specs=(HBM_SPEC,) * 3,
        scratch_shapes=[
            pltpu.VMEM(basis.shape, F32),
            pltpu.VMEM(factor.shape, F32),
            pltpu.VMEM(coeffs.shape, BF16),
            pltpu.VMEM((1, rank, frame_count), F32),
            pltpu.SemaphoreType.DMA((3,)),
            pltpu.SemaphoreType.DMA((3,)),
        ],
        compiler_params=pltpu.CompilerParams(vmem_limit_bytes=GRANT),
        name="finish",
    )(basis, factor, coeffs)


def solution(mesh):
    placed = (P("rows", "batch"), P(), P(), P("batch", None))
    return jax.shard_map(
        shards,
        mesh=mesh,
        in_specs=placed,
        out_specs=(P("batch", "rows", None), P("batch", None, None), P("batch", None, None)),
        check_vma=False,
    )
```

```python
import functools
import math

import jax
import jax.numpy as jnp
from jax import lax
from jax.experimental import pallas as pl
from jax.experimental.pallas import tpu as pltpu
from jax.sharding import PartitionSpec as P

MESH = pl.DeviceIdType.MESH
HIGHEST = lax.Precision.HIGHEST
F32 = jnp.float32
BF16 = jnp.bfloat16
LANES = 128
PANEL = 32
TILE = 8
GRANT = 63 * 1024 * 1024
HBM_SPEC = pl.BlockSpec(memory_space=pltpu.HBM)
VMEM_SPEC = pl.BlockSpec(memory_space=pltpu.VMEM)


def greet(count, batches, with_batch):
    row, turn = lax.axis_index("rows"), lax.axis_index("batch")
    barrier = pltpu.get_barrier_semaphore()
    for step in range(1, count):
        pl.semaphore_signal(
            barrier, inc=1, device_id=(lax.rem(row + step, count), turn), device_id_type=MESH
        )
    waits = count - 1
    if with_batch and batches > 1:

        @pl.when(turn > 0)
        def _():
            pl.semaphore_signal(barrier, inc=1, device_id=(row, turn - 1), device_id_type=MESH)

        @pl.when(turn < batches - 1)
        def _():
            pl.semaphore_signal(barrier, inc=1, device_id=(row, turn + 1), device_id_type=MESH)

        waits = waits + jnp.where(turn > 0, 1, 0) + jnp.where(turn < batches - 1, 1, 0)
    pl.semaphore_wait(barrier, waits)


def exchange(count, source_of, target_of, send_sems, recv_sems):
    row, turn = lax.axis_index("rows"), lax.axis_index("batch")
    copies = []
    for step in range(1, count):
        peer = lax.rem(row + step, count)
        copy = pltpu.make_async_remote_copy(
            src_ref=source_of(peer),
            dst_ref=target_of(row),
            send_sem=send_sems.at[step],
            recv_sem=recv_sems.at[step],
            device_id=(peer, turn),
            device_id_type=MESH,
        )
        copy.start()
        copies.append(copy)
    return copies


def groups(count):
    inner = 4 if count % 4 == 0 else 1
    return count // inner, inner


def send(source, target, send_sems, recv_sems, index, peer):
    copy = pltpu.make_async_remote_copy(
        src_ref=source,
        dst_ref=target,
        send_sem=send_sems.at[index],
        recv_sem=recv_sems.at[index],
        device_id=(peer, lax.axis_index("batch")),
        device_id_type=MESH,
    )
    copy.start()
    return copy


def place_of(count):
    inner = groups(count)[1]
    row = lax.axis_index("rows")
    return lax.div(row, inner), lax.rem(row, inner)


def gather(count, total, send_sems, recv_sems):
    outer, inner = groups(count)
    plane, spot = place_of(count)
    row = lax.axis_index("rows")
    across, within = [], []
    for o in range(1, outer):
        peer = lax.rem(plane + o, outer) * inner + spot
        across.append(send(total.at[row], total.at[row], send_sems, recv_sems, o * inner, peer))
    for o in range(outer):
        if o > 0:
            across[o - 1].wait_recv()
        owner = lax.rem(plane - o + outer, outer) * inner + spot
        for i in range(1, inner):
            peer = plane * inner + lax.rem(spot + i, inner)
            within.append(send(total.at[owner], total.at[owner], send_sems, recv_sems, o * inner + i, peer))
    return across, within


def cut(value, index, shard, dtype):
    low = index * shard
    if low < value.shape[0]:
        return value[low : low + shard]
    return jnp.zeros((shard, value.shape[1]), dtype)


def sum_slots(landed, copies):
    for copy in copies:
        copy.wait_recv()
    summed = landed[0]
    for sender in range(1, landed.shape[0]):
        summed = summed + landed[sender]
    return summed


def whole_kernel(
    count, batches, npoints,
    frames_hbm, taps_hbm, sketch_hbm, rates_hbm, basis_hbm, factor_hbm, coeffs,
    frames, taps, sketch, rates, tap_row, history, before, weighted, filtered,
    parts, landed, total, cross_parts, cross_landed, cross_mid, cross_last, cross_total, work, upper, inverse, basis, factor,
    load_sems, store_sems, hist_sems, prev_sems, gram_a, gram_b, gram_c, gram_d, cross_a, cross_b, cross_c, cross_d, cross_e, cross_f,
):
    row, turn = lax.axis_index("rows"), lax.axis_index("batch")
    frame_count = frames.shape[1]
    rank = sketch.shape[1]
    loads = [
        pltpu.make_async_copy(source, target, load_sems.at[index])
        for index, (source, target) in enumerate(
            ((taps_hbm, taps), (frames_hbm, frames), (sketch_hbm, sketch), (rates_hbm, rates))
        )
    ]
    for load in loads:
        load.start()
    greet(count, batches, True)

    def hist_copy():
        return pltpu.make_async_remote_copy(
            src_ref=frames_hbm.at[:, pl.ds(frame_count - LANES, LANES)],
            dst_ref=history,
            send_sem=hist_sems.at[0],
            recv_sem=hist_sems.at[1],
            device_id=(row, turn + 1),
            device_id_type=MESH,
        )

    def prev_copy():
        return pltpu.make_async_remote_copy(
            src_ref=weighted,
            dst_ref=before,
            send_sem=prev_sems.at[0],
            recv_sem=prev_sems.at[1],
            device_id=(row, turn + 1),
            device_id_type=MESH,
        )

    @pl.when(turn < batches - 1)
    def _():
        hist_copy().start()

    loads[0].wait()
    tap_row[...] = jnp.zeros_like(tap_row)
    tap_row[:, : taps.shape[1]] = taps[...].astype(F32) / 1024.0
    spread = jnp.broadcast_to(tap_row[...], (LANES, tap_row.shape[1]))
    rolled = pltpu.roll(spread, 0, 1, stride=1, stride_axis=0)
    wide = tap_row.shape[1]
    after = jnp.concatenate([rolled[:, wide - LANES :], rolled[:, :LANES]], axis=1)
    band = jnp.concatenate([rolled[:, LANES : 3 * LANES], rolled[:, : 2 * LANES], after], axis=0).astype(BF16)

    step = 2 * LANES
    loads[1].wait()
    for start in range(step, frame_count, step):
        filtered[:, start : start + step] = jnp.dot(
            frames[:, start - LANES : start + step], band, preferred_element_type=F32
        ).astype(BF16)
    here = jnp.dot(frames[:, :step], band[LANES:], preferred_element_type=F32)
    loads[2].wait()
    loads[3].wait()

    @pl.when(turn == 0)
    def _():
        history[...] = jnp.zeros_like(history)

    @pl.when(turn > 0)
    def _():
        hist_copy().wait_recv()

    filtered[:, :step] = (
        here + jnp.dot(history[...], band[:LANES], preferred_element_type=F32)
    ).astype(BF16)
    weighted[...] = jnp.dot(filtered[...], sketch[...], preferred_element_type=F32)

    @pl.when(turn > 0)
    def _():
        prev_copy().wait_recv()
        weighted[...] = rates[...] * before[...] + weighted[...]

    @pl.when(turn < batches - 1)
    def _():
        prev_copy().start()

    value = weighted[...]
    gram = jnp.dot(value.T, value, precision=HIGHEST, preferred_element_type=F32)
    half = rank // 2
    blocks = jnp.concatenate([gram[:half, :half], gram[:half, half:], gram[half:, half:]], axis=0)
    for index in range(count):
        parts[index] = cut(blocks, index, parts.shape[1], F32)
    gram_first = exchange(count, lambda peer: parts.at[peer], lambda mine: landed.at[mine], gram_a, gram_b)

    turned = filtered[...].T
    cross = jnp.zeros((frame_count, rank), F32)
    for piece in reversed(pieces(value)):
        cross = cross + jnp.dot(turned, piece.astype(BF16), preferred_element_type=F32)
    outer, inner = groups(count)
    plane, spot = place_of(count)
    shard = cross_total.shape[1]
    for index in range(count):
        cross_parts[index % inner, index // inner] = cut(cross, index, shard, F32)
    cross_first = []
    for i in range(1, inner):
        other = lax.rem(spot + i, inner)
        cross_first.append(
            send(cross_parts.at[other], cross_landed.at[spot], cross_a, cross_b, i, plane * inner + other)
        )
    cross_landed[spot] = cross_parts[spot]

    landed[row] = parts[row]
    total[row] = sum_slots(landed, gram_first)
    gram_second = exchange(count, lambda peer: total.at[row], lambda mine: total.at[mine], gram_c, gram_d)
    ids = lax.broadcasted_iota(jnp.int32, (rank, rank), 0)
    cols = lax.broadcasted_iota(jnp.int32, (rank, rank), 1)
    upper[...] = jnp.zeros_like(upper)
    inverse[...] = jnp.zeros_like(inverse)
    for copy in gram_second:
        copy.wait_recv()
    cross_mid[...] = sum_slots(cross_landed, cross_first)
    cross_last[plane] = cross_mid[plane]
    cross_second = []
    for o in range(1, outer):
        other = lax.rem(plane + o, outer)
        cross_second.append(
            send(cross_mid.at[other], cross_last.at[plane], cross_c, cross_d, o, other * inner + spot)
        )
    packed = jnp.concatenate([total[index] for index in range(count)], axis=0)
    across = packed[half:rank]
    upper_half = jnp.concatenate([packed[:half], across], axis=1)
    lower_half = jnp.concatenate([across.T, packed[rank : rank + half]], axis=1)
    square = jnp.concatenate([upper_half, lower_half], axis=0)
    diagonal = jnp.where(ids == cols, square, 0.0)
    lane_sums = jnp.sum(diagonal, axis=0, keepdims=True)
    lane_scale = lax.rsqrt(lane_sums)
    row_scale = lax.rsqrt(jnp.sum(diagonal, axis=1, keepdims=True))
    work[:, :rank] = square * row_scale * lane_scale
    work[:, rank:] = jnp.where(ids == cols, row_scale, 0.0)
    for begin in range(0, rank, LANES):
        eliminate(work, upper, inverse, begin)

    root = math.sqrt(npoints)
    against = (((1,), (1,)), ((), ()))
    mine = sum_slots(cross_last, cross_second) * (math.sqrt(rank) / root)
    cross_total[row] = lax.dot_general(
        mine, inverse[...], against, precision=HIGHEST, preferred_element_type=F32
    ).astype(BF16)
    cross_across, cross_within = gather(count, cross_total, cross_e, cross_f)
    factor[0] = jnp.where(cols >= ids, upper[...], 0.0) * (lane_sums * lane_scale * (1.0 / root))
    store_factor = pltpu.make_async_copy(factor, factor_hbm, store_sems.at[0])
    store_factor.start()
    basis[0] = lax.dot_general(
        weighted[...], inverse[...], against, precision=HIGHEST, preferred_element_type=F32
    ) * root
    store_basis = pltpu.make_async_copy(basis, basis_hbm, store_sems.at[1])
    store_basis.start()
    for copy in cross_within:
        copy.wait_recv()
    for index in range(count):
        low = index * shard
        if low < frame_count:
            coeffs[low : low + shard] = cross_total[index]

    store_factor.wait()
    store_basis.wait()
    sent = gram_first + gram_second + cross_first + cross_second + cross_across + cross_within
    for copy in sent:
        copy.wait_send()

    @pl.when(turn < batches - 1)
    def _():
        hist_copy().wait_send()
        prev_copy().wait_send()


def pieces(x):
    high = x.astype(BF16).astype(F32)
    rest = x - high
    mid = rest.astype(BF16).astype(F32)
    return high, mid, rest - mid


def eliminate(work, upper, inverse, begin):
    rank = work.shape[0]
    first = begin
    last = rank + begin + LANES
    width = rank - first
    tiles = PANEL // TILE
    full = (TILE, LANES)

    def wide(x, copies):
        return jnp.concatenate([x] * copies, axis=1)

    def panel(index, _):
        offset = pl.multiple_of(index * PANEL, PANEL)
        rows = pl.ds(pl.multiple_of(begin + offset, PANEL), PANEL)
        block = work[rows, first:last]
        corner = pltpu.roll(block[:, :LANES], lax.rem(LANES - offset, LANES), 1)
        block = jnp.concatenate([block, corner], axis=1)
        copies = block.shape[1] // LANES
        body = [block[b * TILE : (b + 1) * TILE] for b in range(tiles)]
        place = lax.broadcasted_iota(jnp.int32, body[0].shape, 0)
        for c in range(tiles):
            columns = [
                [
                    jnp.broadcast_to(body[b][:, at : at + 1], full)
                    for at in range(last - first + c * TILE, last - first + (c + 1) * TILE)
                ]
                for b in range(c, tiles)
            ]
            held = {
                (i, j): jnp.broadcast_to(columns[0][j][i : i + 1], full)
                for j in range(TILE)
                for i in range(j, TILE)
            }
            lines = [jnp.broadcast_to(body[c][i : i + 1], body[c].shape) for i in range(TILE)]
            result = jnp.zeros_like(body[c])
            for j in range(0, TILE, 2):
                one = lax.rsqrt(held[j, j])
                minor = held[j, j] * held[j + 1, j + 1] - held[j + 1, j] * held[j + 1, j]
                two = held[j, j] * one * lax.rsqrt(minor)
                link = held[j + 1, j] * one
                rest = range(j + 2, TILE)
                near = {i: held[i, j] * one for i in rest}
                far = {i: (held[i, j + 1] - near[i] * link) * two for i in rest}
                for i in rest:
                    for k in range(j + 2, i + 1):
                        held[i, k] = held[i, k] - (near[i] * near[k] + far[i] * far[k])
                top = lines[j] * wide(one, copies)
                under = (lines[j + 1] - wide(link, copies) * top) * wide(two, copies)
                for i in rest:
                    lines[i] = lines[i] - (wide(near[i], copies) * top + wide(far[i], copies) * under)
                for b in range(c + 1, tiles):
                    column = columns[b - c]
                    left = column[j] * one
                    right = (column[j + 1] - left * link) * two
                    for k in rest:
                        column[k] = column[k] - (left * near[k] + right * far[k])
                    body[b] = body[b] - (wide(left, copies) * top + wide(right, copies) * under)
                result = jnp.where(place == j, top, jnp.where(place == j + 1, under, result))
            body[c] = result
        solved = jnp.concatenate(body, axis=0)[:, : last - first]
        upper[rows, first:rank] = solved[:, :width]
        inverse[rows, : begin + LANES] = solved[:, width:]
        high, mid, low = pieces(solved)
        left = jnp.concatenate([high, high, mid, high, mid, low], axis=0)[:, :width].astype(BF16)
        right = jnp.concatenate([high, mid, high, low, mid, high], axis=0).astype(BF16)
        work[first:, first:last] = work[first:, first:last] - lax.dot_general(
            left, right, (((0,), (0,)), ((), ())), preferred_element_type=F32
        )
        return 0

    lax.fori_loop(0, LANES // PANEL, panel, 0)


def finish_kernel(
    basis_in, factor_in, turned_in, basis_out, factor_out, coeffs_out, basis, factor, turned, coeffs, loaded, stored
):
    loads = [
        pltpu.make_async_copy(source, target, loaded.at[index])
        for index, (source, target) in enumerate(((turned_in, turned), (basis_in, basis), (factor_in, factor)))
    ]
    stores = [
        pltpu.make_async_copy(source, target, stored.at[index])
        for index, (source, target) in enumerate(((coeffs, coeffs_out), (basis, basis_out), (factor, factor_out)))
    ]
    for load in loads:
        load.start()
    for index in (1, 2):
        loads[index].wait()
        stores[index].start()
    loads[0].wait()
    coeffs[0] = turned[...].astype(F32).T
    stores[0].start()
    for store in stores:
        store.wait()


def shard_rows(length, count, tile):
    return tile * -(-length // (tile * count))


def shards(frames, tap_table, sketch_matrix, decay_rates):
    count, batches = lax.axis_size("rows"), lax.axis_size("batch")
    rows_here, frame_count = frames.shape
    rank = sketch_matrix.shape[1]
    half = rank // 2
    taps = tap_table.reshape(1, -1)
    gram_slots = pltpu.VMEM((count, shard_rows(3 * half, count, 8), half), F32)
    outer, inner = groups(count)
    shard = shard_rows(frame_count, count, 16)
    cross_slots = pltpu.VMEM((inner, outer, shard, rank), F32)
    cross_line = pltpu.VMEM((outer, shard, rank), F32)
    basis, factor, coeffs = pl.pallas_call(
        functools.partial(whole_kernel, count, batches, rows_here * count),
        out_shape=(
            jax.ShapeDtypeStruct((1, rows_here, rank), F32),
            jax.ShapeDtypeStruct((1, rank, rank), F32),
            jax.ShapeDtypeStruct((frame_count, rank), BF16),
        ),
        in_specs=[HBM_SPEC] * 4,
        out_specs=(HBM_SPEC, HBM_SPEC, VMEM_SPEC),
        scratch_shapes=[
            pltpu.VMEM(frames.shape, BF16),
            pltpu.VMEM(taps.shape, jnp.int32),
            pltpu.VMEM(sketch_matrix.shape, BF16),
            pltpu.VMEM(decay_rates.shape, F32),
            pltpu.VMEM((1, 4 * LANES), F32),
            pltpu.VMEM((rows_here, LANES), BF16),
            pltpu.VMEM((rows_here, rank), F32),
            pltpu.VMEM((rows_here, rank), F32),
            pltpu.VMEM((rows_here, frame_count), BF16),
            gram_slots,
            gram_slots,
            gram_slots,
            cross_slots,
            cross_slots,
            cross_line,
            cross_line,
            pltpu.VMEM((count, shard, rank), BF16),
            pltpu.VMEM((rank, 2 * rank), F32),
            pltpu.VMEM((rank, rank), F32),
            pltpu.VMEM((rank, rank), F32),
            pltpu.VMEM((1, rows_here, rank), F32),
            pltpu.VMEM((1, rank, rank), F32),
            pltpu.SemaphoreType.DMA((4,)),
            pltpu.SemaphoreType.DMA((2,)),
            pltpu.SemaphoreType.DMA((2,)),
            pltpu.SemaphoreType.DMA((2,)),
        ] + [pltpu.SemaphoreType.DMA((count,)) for _ in range(10)],
        compiler_params=pltpu.CompilerParams(
            collective_id=0, has_side_effects=True, vmem_limit_bytes=GRANT
        ),
        name="whole",
    )(frames, taps, sketch_matrix, decay_rates)
    return pl.pallas_call(
        finish_kernel,
        out_shape=(
            jax.ShapeDtypeStruct(basis.shape, F32),
            jax.ShapeDtypeStruct(factor.shape, F32),
            jax.ShapeDtypeStruct((1, rank, frame_count), F32),
        ),
        in_specs=[HBM_SPEC] * 3,
        out_specs=(HBM_SPEC,) * 3,
        scratch_shapes=[
            pltpu.VMEM(basis.shape, F32),
            pltpu.VMEM(factor.shape, F32),
            pltpu.VMEM(coeffs.shape, BF16),
            pltpu.VMEM((1, rank, frame_count), F32),
            pltpu.SemaphoreType.DMA((3,)),
            pltpu.SemaphoreType.DMA((3,)),
        ],
        compiler_params=pltpu.CompilerParams(vmem_limit_bytes=GRANT),
        name="finish",
    )(basis, factor, coeffs)


def solution(mesh):
    placed = (P("rows", "batch"), P(), P(), P("batch", None))
    return jax.shard_map(
        shards,
        mesh=mesh,
        in_specs=placed,
        out_specs=(P("batch", "rows", None), P("batch", None, None), P("batch", None, None)),
        check_vma=False,
    )
```

```python
import functools
import math

import jax
import jax.numpy as jnp
from jax import lax
from jax.experimental import pallas as pl
from jax.experimental.pallas import tpu as pltpu
from jax.sharding import PartitionSpec as P

MESH = pl.DeviceIdType.MESH
HIGHEST = lax.Precision.HIGHEST
F32 = jnp.float32
BF16 = jnp.bfloat16
LANES = 128
PANEL = 32
TILE = 8
GRANT = 63 * 1024 * 1024
HBM_SPEC = pl.BlockSpec(memory_space=pltpu.HBM)
VMEM_SPEC = pl.BlockSpec(memory_space=pltpu.VMEM)


def greet(count, batches, with_batch):
    row, turn = lax.axis_index("rows"), lax.axis_index("batch")
    barrier = pltpu.get_barrier_semaphore()
    for step in range(1, count):
        pl.semaphore_signal(
            barrier, inc=1, device_id=(lax.rem(row + step, count), turn), device_id_type=MESH
        )
    waits = count - 1
    if with_batch and batches > 1:

        @pl.when(turn > 0)
        def _():
            pl.semaphore_signal(barrier, inc=1, device_id=(row, turn - 1), device_id_type=MESH)

        @pl.when(turn < batches - 1)
        def _():
            pl.semaphore_signal(barrier, inc=1, device_id=(row, turn + 1), device_id_type=MESH)

        waits = waits + jnp.where(turn > 0, 1, 0) + jnp.where(turn < batches - 1, 1, 0)
    pl.semaphore_wait(barrier, waits)


def exchange(count, source_of, target_of, send_sems, recv_sems):
    row, turn = lax.axis_index("rows"), lax.axis_index("batch")
    copies = []
    for step in range(1, count):
        peer = lax.rem(row + step, count)
        copy = pltpu.make_async_remote_copy(
            src_ref=source_of(peer),
            dst_ref=target_of(row),
            send_sem=send_sems.at[step],
            recv_sem=recv_sems.at[step],
            device_id=(peer, turn),
            device_id_type=MESH,
        )
        copy.start()
        copies.append(copy)
    return copies


def groups(count):
    inner = 4 if count % 4 == 0 else 1
    return count // inner, inner


def send(source, target, send_sems, recv_sems, index, peer):
    copy = pltpu.make_async_remote_copy(
        src_ref=source,
        dst_ref=target,
        send_sem=send_sems.at[index],
        recv_sem=recv_sems.at[index],
        device_id=(peer, lax.axis_index("batch")),
        device_id_type=MESH,
    )
    copy.start()
    return copy


def place_of(count):
    inner = groups(count)[1]
    row = lax.axis_index("rows")
    return lax.div(row, inner), lax.rem(row, inner)


def gather(count, total, send_sems, recv_sems):
    outer, inner = groups(count)
    plane, spot = place_of(count)
    row = lax.axis_index("rows")
    across, within = [], []
    for o in range(1, outer):
        peer = lax.rem(plane + o, outer) * inner + spot
        across.append(send(total.at[row], total.at[row], send_sems, recv_sems, o * inner, peer))
    for o in range(outer):
        if o > 0:
            across[o - 1].wait_recv()
        owner = lax.rem(plane - o + outer, outer) * inner + spot
        for i in range(1, inner):
            peer = plane * inner + lax.rem(spot + i, inner)
            within.append(send(total.at[owner], total.at[owner], send_sems, recv_sems, o * inner + i, peer))
    return across, within


def cut(value, index, shard, dtype):
    low = index * shard
    if low < value.shape[0]:
        return value[low : low + shard]
    return jnp.zeros((shard, value.shape[1]), dtype)


def sum_slots(landed, copies):
    for copy in copies:
        copy.wait_recv()
    summed = landed[0]
    for sender in range(1, landed.shape[0]):
        summed = summed + landed[sender]
    return summed


def whole_kernel(
    count, batches, npoints,
    frames_hbm, taps_hbm, sketch_hbm, rates_hbm, basis_hbm, factor_hbm, coeffs,
    frames, taps, sketch, rates, tap_row, history, before, weighted, filtered,
    parts, landed, total, cross_parts, cross_landed, cross_mid, cross_last, cross_total, work, upper, inverse, basis, factor,
    load_sems, store_sems, hist_sems, prev_sems, gram_a, gram_b, gram_c, gram_d, cross_a, cross_b, cross_c, cross_d, cross_e, cross_f,
):
    row, turn = lax.axis_index("rows"), lax.axis_index("batch")
    frame_count = frames.shape[1]
    rank = sketch.shape[1]
    loads = [
        pltpu.make_async_copy(source, target, load_sems.at[index])
        for index, (source, target) in enumerate(
            ((taps_hbm, taps), (frames_hbm, frames), (sketch_hbm, sketch), (rates_hbm, rates))
        )
    ]
    for load in loads:
        load.start()
    greet(count, batches, True)

    def hist_copy():
        return pltpu.make_async_remote_copy(
            src_ref=frames_hbm.at[:, pl.ds(frame_count - LANES, LANES)],
            dst_ref=history,
            send_sem=hist_sems.at[0],
            recv_sem=hist_sems.at[1],
            device_id=(row, turn + 1),
            device_id_type=MESH,
        )

    def prev_copy():
        return pltpu.make_async_remote_copy(
            src_ref=weighted,
            dst_ref=before,
            send_sem=prev_sems.at[0],
            recv_sem=prev_sems.at[1],
            device_id=(row, turn + 1),
            device_id_type=MESH,
        )

    @pl.when(turn < batches - 1)
    def _():
        hist_copy().start()

    loads[0].wait()
    tap_row[...] = jnp.zeros_like(tap_row)
    tap_row[:, : taps.shape[1]] = taps[...].astype(F32) / 1024.0
    spread = jnp.broadcast_to(tap_row[...], (LANES, tap_row.shape[1]))
    rolled = pltpu.roll(spread, 0, 1, stride=1, stride_axis=0)
    wide = tap_row.shape[1]
    after = jnp.concatenate([rolled[:, wide - LANES :], rolled[:, :LANES]], axis=1)
    band = jnp.concatenate([rolled[:, LANES : 3 * LANES], rolled[:, : 2 * LANES], after], axis=0).astype(BF16)

    step = 2 * LANES
    loads[1].wait()
    for start in range(step, frame_count, step):
        filtered[:, start : start + step] = jnp.dot(
            frames[:, start - LANES : start + step], band, preferred_element_type=F32
        ).astype(BF16)
    here = jnp.dot(frames[:, :step], band[LANES:], preferred_element_type=F32)
    loads[2].wait()
    loads[3].wait()

    @pl.when(turn == 0)
    def _():
        history[...] = jnp.zeros_like(history)

    @pl.when(turn > 0)
    def _():
        hist_copy().wait_recv()

    filtered[:, :step] = (
        here + jnp.dot(history[...], band[:LANES], preferred_element_type=F32)
    ).astype(BF16)
    weighted[...] = jnp.dot(filtered[...], sketch[...], preferred_element_type=F32)

    @pl.when(turn > 0)
    def _():
        prev_copy().wait_recv()
        weighted[...] = rates[...] * before[...] + weighted[...]

    @pl.when(turn < batches - 1)
    def _():
        prev_copy().start()

    value = weighted[...]
    gram = jnp.dot(value.T, value, precision=HIGHEST, preferred_element_type=F32)
    half = rank // 2
    blocks = jnp.concatenate([gram[:half, :half], gram[:half, half:], gram[half:, half:]], axis=0)
    for index in range(count):
        parts[index] = cut(blocks, index, parts.shape[1], F32)
    gram_first = exchange(count, lambda peer: parts.at[peer], lambda mine: landed.at[mine], gram_a, gram_b)

    turned = filtered[...].T
    cross = jnp.zeros((frame_count, rank), F32)
    for piece in reversed(pieces(value)):
        cross = cross + jnp.dot(turned, piece.astype(BF16), preferred_element_type=F32)
    outer, inner = groups(count)
    plane, spot = place_of(count)
    shard = cross_total.shape[1]
    for index in range(count):
        cross_parts[index % inner, index // inner] = cut(cross, index, shard, F32)
    cross_landed[spot] = cross_parts[spot]

    landed[row] = parts[row]
    total[row] = sum_slots(landed, gram_first)
    gram_second = exchange(count, lambda peer: total.at[row], lambda mine: total.at[mine], gram_c, gram_d)
    cross_first = []
    for i in range(1, inner):
        other = lax.rem(spot + i, inner)
        cross_first.append(
            send(cross_parts.at[other], cross_landed.at[spot], cross_a, cross_b, i, plane * inner + other)
        )
    ids = lax.broadcasted_iota(jnp.int32, (rank, rank), 0)
    cols = lax.broadcasted_iota(jnp.int32, (rank, rank), 1)
    upper[...] = jnp.zeros_like(upper)
    inverse[...] = jnp.zeros_like(inverse)
    for copy in gram_second:
        copy.wait_recv()
    packed = jnp.concatenate([total[index] for index in range(count)], axis=0)
    across = packed[half:rank]
    upper_half = jnp.concatenate([packed[:half], across], axis=1)
    lower_half = jnp.concatenate([across.T, packed[rank : rank + half]], axis=1)
    square = jnp.concatenate([upper_half, lower_half], axis=0)
    diagonal = jnp.where(ids == cols, square, 0.0)
    lane_sums = jnp.sum(diagonal, axis=0, keepdims=True)
    lane_scale = lax.rsqrt(lane_sums)
    row_scale = lax.rsqrt(jnp.sum(diagonal, axis=1, keepdims=True))
    work[:, :rank] = square * row_scale * lane_scale
    work[:, rank:] = jnp.where(ids == cols, row_scale, 0.0)
    eliminate(work, upper, inverse, 0)
    cross_mid[...] = sum_slots(cross_landed, cross_first)
    cross_last[plane] = cross_mid[plane]
    cross_second = []
    for o in range(1, outer):
        other = lax.rem(plane + o, outer)
        cross_second.append(
            send(cross_mid.at[other], cross_last.at[plane], cross_c, cross_d, o, other * inner + spot)
        )
    for begin in range(LANES, rank, LANES):
        eliminate(work, upper, inverse, begin)

    root = math.sqrt(npoints)
    against = (((1,), (1,)), ((), ()))
    mine = sum_slots(cross_last, cross_second) * (math.sqrt(rank) / root)
    cross_total[row] = lax.dot_general(
        mine, inverse[...], against, precision=HIGHEST, preferred_element_type=F32
    ).astype(BF16)
    cross_across, cross_within = gather(count, cross_total, cross_e, cross_f)
    factor[0] = jnp.where(cols >= ids, upper[...], 0.0) * (lane_sums * lane_scale * (1.0 / root))
    store_factor = pltpu.make_async_copy(factor, factor_hbm, store_sems.at[0])
    store_factor.start()
    basis[0] = lax.dot_general(
        weighted[...], inverse[...], against, precision=HIGHEST, preferred_element_type=F32
    ) * root
    store_basis = pltpu.make_async_copy(basis, basis_hbm, store_sems.at[1])
    store_basis.start()
    for copy in cross_within:
        copy.wait_recv()
    for index in range(count):
        low = index * shard
        if low < frame_count:
            coeffs[low : low + shard] = cross_total[index]

    store_factor.wait()
    store_basis.wait()
    sent = gram_first + gram_second + cross_first + cross_second + cross_across + cross_within
    for copy in sent:
        copy.wait_send()

    @pl.when(turn < batches - 1)
    def _():
        hist_copy().wait_send()
        prev_copy().wait_send()


def pieces(x):
    high = x.astype(BF16).astype(F32)
    rest = x - high
    mid = rest.astype(BF16).astype(F32)
    return high, mid, rest - mid


def eliminate(work, upper, inverse, begin):
    rank = work.shape[0]
    first = begin
    last = rank + begin + LANES
    width = rank - first
    tiles = PANEL // TILE
    full = (TILE, LANES)

    def wide(x, copies):
        return jnp.concatenate([x] * copies, axis=1)

    def panel(index, _):
        offset = pl.multiple_of(index * PANEL, PANEL)
        rows = pl.ds(pl.multiple_of(begin + offset, PANEL), PANEL)
        block = work[rows, first:last]
        corner = pltpu.roll(block[:, :LANES], lax.rem(LANES - offset, LANES), 1)
        block = jnp.concatenate([block, corner], axis=1)
        copies = block.shape[1] // LANES
        body = [block[b * TILE : (b + 1) * TILE] for b in range(tiles)]
        place = lax.broadcasted_iota(jnp.int32, body[0].shape, 0)
        for c in range(tiles):
            columns = [
                [
                    jnp.broadcast_to(body[b][:, at : at + 1], full)
                    for at in range(last - first + c * TILE, last - first + (c + 1) * TILE)
                ]
                for b in range(c, tiles)
            ]
            held = {
                (i, j): jnp.broadcast_to(columns[0][j][i : i + 1], full)
                for j in range(TILE)
                for i in range(j, TILE)
            }
            lines = [jnp.broadcast_to(body[c][i : i + 1], body[c].shape) for i in range(TILE)]
            result = jnp.zeros_like(body[c])
            for j in range(0, TILE, 2):
                one = lax.rsqrt(held[j, j])
                minor = held[j, j] * held[j + 1, j + 1] - held[j + 1, j] * held[j + 1, j]
                two = held[j, j] * one * lax.rsqrt(minor)
                link = held[j + 1, j] * one
                rest = range(j + 2, TILE)
                near = {i: held[i, j] * one for i in rest}
                far = {i: (held[i, j + 1] - near[i] * link) * two for i in rest}
                for i in rest:
                    for k in range(j + 2, i + 1):
                        held[i, k] = held[i, k] - (near[i] * near[k] + far[i] * far[k])
                top = lines[j] * wide(one, copies)
                under = (lines[j + 1] - wide(link, copies) * top) * wide(two, copies)
                for i in rest:
                    lines[i] = lines[i] - (wide(near[i], copies) * top + wide(far[i], copies) * under)
                for b in range(c + 1, tiles):
                    column = columns[b - c]
                    left = column[j] * one
                    right = (column[j + 1] - left * link) * two
                    for k in rest:
                        column[k] = column[k] - (left * near[k] + right * far[k])
                    body[b] = body[b] - (wide(left, copies) * top + wide(right, copies) * under)
                result = jnp.where(place == j, top, jnp.where(place == j + 1, under, result))
            body[c] = result
        solved = jnp.concatenate(body, axis=0)[:, : last - first]
        upper[rows, first:rank] = solved[:, :width]
        inverse[rows, : begin + LANES] = solved[:, width:]
        high, mid, low = pieces(solved)
        left = jnp.concatenate([high, high, mid, high, mid, low], axis=0)[:, :width].astype(BF16)
        right = jnp.concatenate([high, mid, high, low, mid, high], axis=0).astype(BF16)
        work[first:, first:last] = work[first:, first:last] - lax.dot_general(
            left, right, (((0,), (0,)), ((), ())), preferred_element_type=F32
        )
        return 0

    lax.fori_loop(0, LANES // PANEL, panel, 0)


def finish_kernel(
    basis_in, factor_in, turned_in, basis_out, factor_out, coeffs_out, basis, factor, turned, coeffs, loaded, stored
):
    loads = [
        pltpu.make_async_copy(source, target, loaded.at[index])
        for index, (source, target) in enumerate(((turned_in, turned), (basis_in, basis), (factor_in, factor)))
    ]
    stores = [
        pltpu.make_async_copy(source, target, stored.at[index])
        for index, (source, target) in enumerate(((coeffs, coeffs_out), (basis, basis_out), (factor, factor_out)))
    ]
    for load in loads:
        load.start()
    for index in (1, 2):
        loads[index].wait()
        stores[index].start()
    loads[0].wait()
    coeffs[0] = turned[...].astype(F32).T
    stores[0].start()
    for store in stores:
        store.wait()


def shard_rows(length, count, tile):
    return tile * -(-length // (tile * count))


def shards(frames, tap_table, sketch_matrix, decay_rates):
    count, batches = lax.axis_size("rows"), lax.axis_size("batch")
    rows_here, frame_count = frames.shape
    rank = sketch_matrix.shape[1]
    half = rank // 2
    taps = tap_table.reshape(1, -1)
    gram_slots = pltpu.VMEM((count, shard_rows(3 * half, count, 8), half), F32)
    outer, inner = groups(count)
    shard = shard_rows(frame_count, count, 16)
    cross_slots = pltpu.VMEM((inner, outer, shard, rank), F32)
    cross_line = pltpu.VMEM((outer, shard, rank), F32)
    basis, factor, coeffs = pl.pallas_call(
        functools.partial(whole_kernel, count, batches, rows_here * count),
        out_shape=(
            jax.ShapeDtypeStruct((1, rows_here, rank), F32),
            jax.ShapeDtypeStruct((1, rank, rank), F32),
            jax.ShapeDtypeStruct((frame_count, rank), BF16),
        ),
        in_specs=[HBM_SPEC] * 4,
        out_specs=(HBM_SPEC, HBM_SPEC, VMEM_SPEC),
        scratch_shapes=[
            pltpu.VMEM(frames.shape, BF16),
            pltpu.VMEM(taps.shape, jnp.int32),
            pltpu.VMEM(sketch_matrix.shape, BF16),
            pltpu.VMEM(decay_rates.shape, F32),
            pltpu.VMEM((1, 4 * LANES), F32),
            pltpu.VMEM((rows_here, LANES), BF16),
            pltpu.VMEM((rows_here, rank), F32),
            pltpu.VMEM((rows_here, rank), F32),
            pltpu.VMEM((rows_here, frame_count), BF16),
            gram_slots,
            gram_slots,
            gram_slots,
            cross_slots,
            cross_slots,
            cross_line,
            cross_line,
            pltpu.VMEM((count, shard, rank), BF16),
            pltpu.VMEM((rank, 2 * rank), F32),
            pltpu.VMEM((rank, rank), F32),
            pltpu.VMEM((rank, rank), F32),
            pltpu.VMEM((1, rows_here, rank), F32),
            pltpu.VMEM((1, rank, rank), F32),
            pltpu.SemaphoreType.DMA((4,)),
            pltpu.SemaphoreType.DMA((2,)),
            pltpu.SemaphoreType.DMA((2,)),
            pltpu.SemaphoreType.DMA((2,)),
        ] + [pltpu.SemaphoreType.DMA((count,)) for _ in range(10)],
        compiler_params=pltpu.CompilerParams(
            collective_id=0, has_side_effects=True, vmem_limit_bytes=GRANT
        ),
        name="whole",
    )(frames, taps, sketch_matrix, decay_rates)
    return pl.pallas_call(
        finish_kernel,
        out_shape=(
            jax.ShapeDtypeStruct(basis.shape, F32),
            jax.ShapeDtypeStruct(factor.shape, F32),
            jax.ShapeDtypeStruct((1, rank, frame_count), F32),
        ),
        in_specs=[HBM_SPEC] * 3,
        out_specs=(HBM_SPEC,) * 3,
        scratch_shapes=[
            pltpu.VMEM(basis.shape, F32),
            pltpu.VMEM(factor.shape, F32),
            pltpu.VMEM(coeffs.shape, BF16),
            pltpu.VMEM((1, rank, frame_count), F32),
            pltpu.SemaphoreType.DMA((3,)),
            pltpu.SemaphoreType.DMA((3,)),
        ],
        compiler_params=pltpu.CompilerParams(vmem_limit_bytes=GRANT),
        name="finish",
    )(basis, factor, coeffs)


def solution(mesh):
    placed = (P("rows", "batch"), P(), P(), P("batch", None))
    return jax.shard_map(
        shards,
        mesh=mesh,
        in_specs=placed,
        out_specs=(P("batch", "rows", None), P("batch", None, None), P("batch", None, None)),
        check_vma=False,
    )
```

```python
import functools
import math

import jax
import jax.numpy as jnp
from jax import lax
from jax.experimental import pallas as pl
from jax.experimental.pallas import tpu as pltpu
from jax.sharding import PartitionSpec as P

MESH = pl.DeviceIdType.MESH
HIGHEST = lax.Precision.HIGHEST
F32 = jnp.float32
BF16 = jnp.bfloat16
LANES = 128
PANEL = 32
TILE = 8
GRANT = 63 * 1024 * 1024
HBM_SPEC = pl.BlockSpec(memory_space=pltpu.HBM)
VMEM_SPEC = pl.BlockSpec(memory_space=pltpu.VMEM)


def greet(count, batches, with_batch):
    row, turn = lax.axis_index("rows"), lax.axis_index("batch")
    barrier = pltpu.get_barrier_semaphore()
    for step in range(1, count):
        pl.semaphore_signal(
            barrier, inc=1, device_id=(lax.rem(row + step, count), turn), device_id_type=MESH
        )
    waits = count - 1
    if with_batch and batches > 1:

        @pl.when(turn > 0)
        def _():
            pl.semaphore_signal(barrier, inc=1, device_id=(row, turn - 1), device_id_type=MESH)

        @pl.when(turn < batches - 1)
        def _():
            pl.semaphore_signal(barrier, inc=1, device_id=(row, turn + 1), device_id_type=MESH)

        waits = waits + jnp.where(turn > 0, 1, 0) + jnp.where(turn < batches - 1, 1, 0)
    pl.semaphore_wait(barrier, waits)


def exchange(count, source_of, target_of, send_sems, recv_sems):
    row, turn = lax.axis_index("rows"), lax.axis_index("batch")
    copies = []
    for step in range(1, count):
        peer = lax.rem(row + step, count)
        copy = pltpu.make_async_remote_copy(
            src_ref=source_of(peer),
            dst_ref=target_of(row),
            send_sem=send_sems.at[step],
            recv_sem=recv_sems.at[step],
            device_id=(peer, turn),
            device_id_type=MESH,
        )
        copy.start()
        copies.append(copy)
    return copies


def groups(count):
    inner = 4 if count % 4 == 0 else 1
    return count // inner, inner


def send(source, target, send_sems, recv_sems, index, peer):
    copy = pltpu.make_async_remote_copy(
        src_ref=source,
        dst_ref=target,
        send_sem=send_sems.at[index],
        recv_sem=recv_sems.at[index],
        device_id=(peer, lax.axis_index("batch")),
        device_id_type=MESH,
    )
    copy.start()
    return copy


def place_of(count):
    inner = groups(count)[1]
    row = lax.axis_index("rows")
    return lax.div(row, inner), lax.rem(row, inner)


def cut(value, index, shard, dtype):
    low = index * shard
    if low < value.shape[0]:
        return value[low : low + shard]
    return jnp.zeros((shard, value.shape[1]), dtype)


def sum_slots(landed, copies):
    for copy in copies:
        copy.wait_recv()
    summed = landed[0]
    for sender in range(1, landed.shape[0]):
        summed = summed + landed[sender]
    return summed


def whole_kernel(
    count, batches, npoints,
    frames_hbm, taps_hbm, sketch_hbm, rates_hbm, basis_hbm, factor_hbm, coeffs,
    frames, taps, sketch, rates, tap_row, history, before, weighted, filtered,
    parts, landed, total, cross_parts, cross_landed, cross_mid, cross_last, cross_total, work, upper, inverse, basis, factor,
    load_sems, store_sems, hist_sems, prev_sems, gram_a, gram_b, gram_c, gram_d, cross_a, cross_b, cross_c, cross_d, cross_e, cross_f,
):
    row, turn = lax.axis_index("rows"), lax.axis_index("batch")
    frame_count = frames.shape[1]
    rank = sketch.shape[1]
    loads = [
        pltpu.make_async_copy(source, target, load_sems.at[index])
        for index, (source, target) in enumerate(
            ((taps_hbm, taps), (frames_hbm, frames), (sketch_hbm, sketch), (rates_hbm, rates))
        )
    ]
    for load in loads:
        load.start()
    greet(count, batches, True)

    def hist_copy():
        return pltpu.make_async_remote_copy(
            src_ref=frames_hbm.at[:, pl.ds(frame_count - LANES, LANES)],
            dst_ref=history,
            send_sem=hist_sems.at[0],
            recv_sem=hist_sems.at[1],
            device_id=(row, turn + 1),
            device_id_type=MESH,
        )

    def prev_copy():
        return pltpu.make_async_remote_copy(
            src_ref=weighted,
            dst_ref=before,
            send_sem=prev_sems.at[0],
            recv_sem=prev_sems.at[1],
            device_id=(row, turn + 1),
            device_id_type=MESH,
        )

    @pl.when(turn < batches - 1)
    def _():
        hist_copy().start()

    loads[0].wait()
    tap_row[...] = jnp.zeros_like(tap_row)
    tap_row[:, : taps.shape[1]] = taps[...].astype(F32) / 1024.0
    spread = jnp.broadcast_to(tap_row[...], (LANES, tap_row.shape[1]))
    rolled = pltpu.roll(spread, 0, 1, stride=1, stride_axis=0)
    wide = tap_row.shape[1]
    after = jnp.concatenate([rolled[:, wide - LANES :], rolled[:, :LANES]], axis=1)
    band = jnp.concatenate([rolled[:, LANES : 3 * LANES], rolled[:, : 2 * LANES], after], axis=0).astype(BF16)

    step = 2 * LANES
    loads[1].wait()
    for start in range(step, frame_count, step):
        filtered[:, start : start + step] = jnp.dot(
            frames[:, start - LANES : start + step], band, preferred_element_type=F32
        ).astype(BF16)
    here = jnp.dot(frames[:, :step], band[LANES:], preferred_element_type=F32)
    loads[2].wait()
    loads[3].wait()

    @pl.when(turn == 0)
    def _():
        history[...] = jnp.zeros_like(history)

    @pl.when(turn > 0)
    def _():
        hist_copy().wait_recv()

    filtered[:, :step] = (
        here + jnp.dot(history[...], band[:LANES], preferred_element_type=F32)
    ).astype(BF16)
    weighted[...] = jnp.dot(filtered[...], sketch[...], preferred_element_type=F32)

    @pl.when(turn > 0)
    def _():
        prev_copy().wait_recv()
        weighted[...] = rates[...] * before[...] + weighted[...]

    @pl.when(turn < batches - 1)
    def _():
        prev_copy().start()

    value = weighted[...]
    gram = jnp.dot(value.T, value, precision=HIGHEST, preferred_element_type=F32)
    half = rank // 2
    blocks = jnp.concatenate([gram[:half, :half], gram[:half, half:], gram[half:, half:]], axis=0)
    for index in range(count):
        parts[index] = cut(blocks, index, parts.shape[1], F32)
    gram_first = exchange(count, lambda peer: parts.at[peer], lambda mine: landed.at[mine], gram_a, gram_b)

    turned = filtered[...].T
    cross = jnp.zeros((frame_count, rank), F32)
    for piece in reversed(pieces(value)):
        cross = cross + jnp.dot(turned, piece.astype(BF16), preferred_element_type=F32)
    outer, inner = groups(count)
    plane, spot = place_of(count)
    shard = cross_total.shape[1]
    for index in range(count):
        cross_parts[index % inner, index // inner] = cut(cross, index, shard, F32)
    cross_first = []
    for i in range(1, inner):
        other = lax.rem(spot + i, inner)
        cross_first.append(
            send(cross_parts.at[other], cross_landed.at[spot], cross_a, cross_b, i, plane * inner + other)
        )
    cross_landed[spot] = cross_parts[spot]

    landed[row] = parts[row]
    total[row] = sum_slots(landed, gram_first)
    gram_second = exchange(count, lambda peer: total.at[row], lambda mine: total.at[mine], gram_c, gram_d)
    ids = lax.broadcasted_iota(jnp.int32, (rank, rank), 0)
    cols = lax.broadcasted_iota(jnp.int32, (rank, rank), 1)
    upper[...] = jnp.zeros_like(upper)
    inverse[...] = jnp.zeros_like(inverse)
    for copy in gram_second:
        copy.wait_recv()
    cross_mid[...] = sum_slots(cross_landed, cross_first)
    cross_last[plane] = cross_mid[plane]
    cross_second = []
    for o in range(1, outer):
        other = lax.rem(plane + o, outer)
        cross_second.append(
            send(cross_mid.at[other], cross_last.at[plane], cross_c, cross_d, o, other * inner + spot)
        )
    packed = jnp.concatenate([total[index] for index in range(count)], axis=0)
    across = packed[half:rank]
    upper_half = jnp.concatenate([packed[:half], across], axis=1)
    lower_half = jnp.concatenate([across.T, packed[rank : rank + half]], axis=1)
    square = jnp.concatenate([upper_half, lower_half], axis=0)
    diagonal = jnp.where(ids == cols, square, 0.0)
    lane_sums = jnp.sum(diagonal, axis=0, keepdims=True)
    lane_scale = lax.rsqrt(lane_sums)
    row_scale = lax.rsqrt(jnp.sum(diagonal, axis=1, keepdims=True))
    work[:, :rank] = square * row_scale * lane_scale
    work[:, rank:] = jnp.where(ids == cols, row_scale, 0.0)
    for begin in range(0, rank, LANES):
        eliminate(work, upper, inverse, begin)

    root = math.sqrt(npoints)
    against = (((1,), (1,)), ((), ()))
    mine = sum_slots(cross_last, cross_second) * (math.sqrt(rank) / root)
    cross_total[row] = lax.dot_general(
        mine, inverse[...], against, precision=HIGHEST, preferred_element_type=F32
    ).astype(BF16)
    cross_third = exchange(
        count, lambda peer: cross_total.at[row], lambda mine: cross_total.at[mine], cross_e, cross_f
    )
    factor[0] = jnp.where(cols >= ids, upper[...], 0.0) * (lane_sums * lane_scale * (1.0 / root))
    store_factor = pltpu.make_async_copy(factor, factor_hbm, store_sems.at[0])
    store_factor.start()
    basis[0] = lax.dot_general(
        weighted[...], inverse[...], against, precision=HIGHEST, preferred_element_type=F32
    ) * root
    store_basis = pltpu.make_async_copy(basis, basis_hbm, store_sems.at[1])
    store_basis.start()
    for copy in cross_third:
        copy.wait_recv()
    for index in range(count):
        low = index * shard
        if low < frame_count:
            coeffs[low : low + shard] = cross_total[index]

    store_factor.wait()
    store_basis.wait()
    sent = gram_first + gram_second + cross_first + cross_second + cross_third
    for copy in sent:
        copy.wait_send()

    @pl.when(turn < batches - 1)
    def _():
        hist_copy().wait_send()
        prev_copy().wait_send()


def pieces(x):
    high = x.astype(BF16).astype(F32)
    rest = x - high
    mid = rest.astype(BF16).astype(F32)
    return high, mid, rest - mid


def eliminate(work, upper, inverse, begin):
    rank = work.shape[0]
    first = begin
    last = rank + begin + LANES
    width = rank - first
    tiles = PANEL // TILE
    full = (TILE, LANES)

    def wide(x, copies):
        return jnp.concatenate([x] * copies, axis=1)

    def panel(index, _):
        offset = pl.multiple_of(index * PANEL, PANEL)
        rows = pl.ds(pl.multiple_of(begin + offset, PANEL), PANEL)
        block = work[rows, first:last]
        corner = pltpu.roll(block[:, :LANES], lax.rem(LANES - offset, LANES), 1)
        block = jnp.concatenate([block, corner], axis=1)
        copies = block.shape[1] // LANES
        body = [block[b * TILE : (b + 1) * TILE] for b in range(tiles)]
        place = lax.broadcasted_iota(jnp.int32, body[0].shape, 0)
        for c in range(tiles):
            columns = [
                [
                    jnp.broadcast_to(body[b][:, at : at + 1], full)
                    for at in range(last - first + c * TILE, last - first + (c + 1) * TILE)
                ]
                for b in range(c, tiles)
            ]
            held = {
                (i, j): jnp.broadcast_to(columns[0][j][i : i + 1], full)
                for j in range(TILE)
                for i in range(j, TILE)
            }
            lines = [jnp.broadcast_to(body[c][i : i + 1], body[c].shape) for i in range(TILE)]
            result = jnp.zeros_like(body[c])
            for j in range(0, TILE, 2):
                one = lax.rsqrt(held[j, j])
                minor = held[j, j] * held[j + 1, j + 1] - held[j + 1, j] * held[j + 1, j]
                two = held[j, j] * one * lax.rsqrt(minor)
                link = held[j + 1, j] * one
                rest = range(j + 2, TILE)
                near = {i: held[i, j] * one for i in rest}
                far = {i: (held[i, j + 1] - near[i] * link) * two for i in rest}
                for i in rest:
                    for k in range(j + 2, i + 1):
                        held[i, k] = held[i, k] - (near[i] * near[k] + far[i] * far[k])
                top = lines[j] * wide(one, copies)
                under = (lines[j + 1] - wide(link, copies) * top) * wide(two, copies)
                for i in rest:
                    lines[i] = lines[i] - (wide(near[i], copies) * top + wide(far[i], copies) * under)
                for b in range(c + 1, tiles):
                    column = columns[b - c]
                    left = column[j] * one
                    right = (column[j + 1] - left * link) * two
                    for k in rest:
                        column[k] = column[k] - (left * near[k] + right * far[k])
                    body[b] = body[b] - (wide(left, copies) * top + wide(right, copies) * under)
                result = jnp.where(place == j, top, jnp.where(place == j + 1, under, result))
            body[c] = result
        solved = jnp.concatenate(body, axis=0)[:, : last - first]
        upper[rows, first:rank] = solved[:, :width]
        inverse[rows, : begin + LANES] = solved[:, width:]
        high, mid, low = pieces(solved)
        left = jnp.concatenate([high, high, mid, high, mid, low], axis=0)[:, :width].astype(BF16)
        right = jnp.concatenate([high, mid, high, low, mid, high], axis=0).astype(BF16)
        work[first:, first:last] = work[first:, first:last] - lax.dot_general(
            left, right, (((0,), (0,)), ((), ())), preferred_element_type=F32
        )
        return 0

    lax.fori_loop(0, LANES // PANEL, panel, 0)


def finish_kernel(
    basis_in, factor_in, turned_in, basis_out, factor_out, coeffs_out, basis, factor, turned, coeffs, loaded, stored
):
    loads = [
        pltpu.make_async_copy(source, target, loaded.at[index])
        for index, (source, target) in enumerate(((turned_in, turned), (basis_in, basis), (factor_in, factor)))
    ]
    stores = [
        pltpu.make_async_copy(source, target, stored.at[index])
        for index, (source, target) in enumerate(((coeffs, coeffs_out), (basis, basis_out), (factor, factor_out)))
    ]
    for load in loads:
        load.start()
    for index in (1, 2):
        loads[index].wait()
        stores[index].start()
    loads[0].wait()
    coeffs[0] = turned[...].astype(F32).T
    stores[0].start()
    for store in stores:
        store.wait()


def shard_rows(length, count, tile):
    return tile * -(-length // (tile * count))


def shards(frames, tap_table, sketch_matrix, decay_rates):
    count, batches = lax.axis_size("rows"), lax.axis_size("batch")
    rows_here, frame_count = frames.shape
    rank = sketch_matrix.shape[1]
    half = rank // 2
    taps = tap_table.reshape(1, -1)
    gram_slots = pltpu.VMEM((count, shard_rows(3 * half, count, 8), half), F32)
    outer, inner = groups(count)
    shard = shard_rows(frame_count, count, 16)
    cross_slots = pltpu.VMEM((inner, outer, shard, rank), F32)
    cross_line = pltpu.VMEM((outer, shard, rank), F32)
    basis, factor, coeffs = pl.pallas_call(
        functools.partial(whole_kernel, count, batches, rows_here * count),
        out_shape=(
            jax.ShapeDtypeStruct((1, rows_here, rank), F32),
            jax.ShapeDtypeStruct((1, rank, rank), F32),
            jax.ShapeDtypeStruct((frame_count, rank), BF16),
        ),
        in_specs=[HBM_SPEC] * 4,
        out_specs=(HBM_SPEC, HBM_SPEC, VMEM_SPEC),
        scratch_shapes=[
            pltpu.VMEM(frames.shape, BF16),
            pltpu.VMEM(taps.shape, jnp.int32),
            pltpu.VMEM(sketch_matrix.shape, BF16),
            pltpu.VMEM(decay_rates.shape, F32),
            pltpu.VMEM((1, 4 * LANES), F32),
            pltpu.VMEM((rows_here, LANES), BF16),
            pltpu.VMEM((rows_here, rank), F32),
            pltpu.VMEM((rows_here, rank), F32),
            pltpu.VMEM((rows_here, frame_count), BF16),
            gram_slots,
            gram_slots,
            gram_slots,
            cross_slots,
            cross_slots,
            cross_line,
            cross_line,
            pltpu.VMEM((count, shard, rank), BF16),
            pltpu.VMEM((rank, 2 * rank), F32),
            pltpu.VMEM((rank, rank), F32),
            pltpu.VMEM((rank, rank), F32),
            pltpu.VMEM((1, rows_here, rank), F32),
            pltpu.VMEM((1, rank, rank), F32),
            pltpu.SemaphoreType.DMA((4,)),
            pltpu.SemaphoreType.DMA((2,)),
            pltpu.SemaphoreType.DMA((2,)),
            pltpu.SemaphoreType.DMA((2,)),
        ] + [pltpu.SemaphoreType.DMA((count,)) for _ in range(10)],
        compiler_params=pltpu.CompilerParams(
            collective_id=0, has_side_effects=True, vmem_limit_bytes=GRANT
        ),
        name="whole",
    )(frames, taps, sketch_matrix, decay_rates)
    return pl.pallas_call(
        finish_kernel,
        out_shape=(
            jax.ShapeDtypeStruct(basis.shape, F32),
            jax.ShapeDtypeStruct(factor.shape, F32),
            jax.ShapeDtypeStruct((1, rank, frame_count), F32),
        ),
        in_specs=[HBM_SPEC] * 3,
        out_specs=(HBM_SPEC,) * 3,
        scratch_shapes=[
            pltpu.VMEM(basis.shape, F32),
            pltpu.VMEM(factor.shape, F32),
            pltpu.VMEM(coeffs.shape, BF16),
            pltpu.VMEM((1, rank, frame_count), F32),
            pltpu.SemaphoreType.DMA((3,)),
            pltpu.SemaphoreType.DMA((3,)),
        ],
        compiler_params=pltpu.CompilerParams(vmem_limit_bytes=GRANT),
        name="finish",
    )(basis, factor, coeffs)


def solution(mesh):
    placed = (P("rows", "batch"), P(), P(), P("batch", None))
    return jax.shard_map(
        shards,
        mesh=mesh,
        in_specs=placed,
        out_specs=(P("batch", "rows", None), P("batch", None, None), P("batch", None, None)),
        check_vma=False,
    )
```
